512 devices in a mesh: row: 16 (over y, core), col: 32 (over x, z).
Axes of the slice: x: 4, y: 8, z: 8, core: 2. Of those that a mesh axis runs over, the one named last changes fastest.
Arguments:
- lam: float32 [14400, 2400], P('row', 'col'), may hold values from -6 to 6
- cycle: float32 [2400, 24000], P('row', 'col'), may hold values from -0.125 to 0.125
- eps_occ: float32 [200], replicated, may hold values from -2 to -0.3
- eps_vir: float32 [1200], replicated, may hold values from 0.1 to 3
- occ_irrep: int32 [200], replicated, may hold values from 0 to 7
- slab: int32 [12], replicated, may hold values from 0 to 199, as said below
- pair_occ: int32 [20], replicated, may hold values from 0 to 199, as said below
- irrep_start: int32 [8], replicated, may hold values from 0 to 1125, as said below
Outputs:
- update: float32 [14400, 24000], P('row', 'col')
The draws below stay inside these ranges and needn't reach their ends.
Inputs may be any that keep to these rules, and one draw needn't show every extreme that they name: `irrep_start`: entry 0 is 0 and the entries rise strictly, so each irrep holds one or more virtual orbitals; the last entry is 1125; sizes may differ. `slab`: distinct occupied orbitals. `pair_occ`: distinct occupied orbitals.
All inputs are finite; a program needn't handle non-finite values.
Results may differ from the reference program's by a relative error of at most 0.000073.
Values sent between devices are 32-bit elements; how exact they have to be, the bound alone decides.
A program may use at most 128 MiB of HBM per device.

```python
import jax
import jax.numpy as jnp
from jax import lax

V = 1200
NOCC = 200
NIRR = 8
SLAB = 12
JO = 20
ROWS = 14400
INNER = 2400
OUTER = 24000


def draw_irrep_start(key, part):
    last_start = V - V // (2 * NIRR)
    cuts = jax.random.permutation(jax.random.fold_in(key, 17), last_start - 1)[:NIRR - 2] + 1
    cuts = jnp.sort(cuts.astype(jnp.int32))
    head = jnp.zeros((1,), jnp.int32)
    tail = jnp.full((1,), last_start, jnp.int32)
    return jnp.concatenate([head, cuts, tail]).astype(jnp.int32)


def draw_slab(key, part):
    return jax.random.permutation(jax.random.fold_in(key, 29), NOCC)[:SLAB].astype(jnp.int32)


def draw_pair_occ(key, part):
    return jax.random.permutation(jax.random.fold_in(key, 41), NOCC)[:JO].astype(jnp.int32)


def place_ends(array, stream_key, least, high):
    longest = array.shape.index(max(array.shape))
    spots = []
    for shift in (0, 1):
        where = [jax.random.randint(jax.random.fold_in(stream_key, axis), (), 0, length) for axis, length in enumerate(array.shape)]
        where[longest] = (where[longest] + shift) % array.shape[longest]
        spots.append(tuple(where))
    return array.at[spots[0]].set(least).at[spots[1]].set(high)


def level_of(own_key, extent, shards, smallest, top_value):
    gain = 1.0
    for position, blocks in shards:
        steps = jax.random.uniform(jax.random.fold_in(jax.random.fold_in(own_key, 6), position), (blocks,), jnp.float32, smallest / len(shards), top_value / len(shards))
        gain = gain * jnp.repeat(jnp.exp(steps), extent[position] // blocks).reshape((-1,) + (1,) * (len(extent) - 1 - position))
    return gain


def noise(stream_key, extent, width, reach, split=(), held_as=jnp.bfloat16):
    array = width * jax.random.normal(stream_key, extent, jnp.float32)
    if split:
        array = array * level_of(stream_key, extent, split, -0.22, 0.18)
    return jnp.clip(array, -reach, reach).astype(held_as)


def setup_inputs(seed: int = 0) -> dict:
    arg_keys = jax.random.split(jax.random.key(seed), 9)
    lam = noise(arg_keys[0], (ROWS, INNER), 1.0, 6.0, ((0, 16), (1, 32)), jnp.float32)
    cycle = noise(arg_keys[1], (INNER, OUTER), INNER ** -0.5, 0.125, ((0, 16), (1, 32)), jnp.float32)
    eps_occ = jnp.clip(jax.random.uniform(arg_keys[2], (NOCC,), jnp.float32, -2.0, -0.3), -2.0, -0.3)
    eps_vir = jnp.clip(jax.random.uniform(arg_keys[3], (V,), jnp.float32, 0.1, 3.0), 0.1, 3.0)
    occ_irrep = place_ends(jax.random.randint(arg_keys[4], (NOCC,), 0, NIRR), jax.random.fold_in(arg_keys[4], 1), 0, NIRR - 1).astype(jnp.int32)
    slab = draw_slab(jax.random.fold_in(arg_keys[8], 71), 0)
    pair_occ = draw_pair_occ(jax.random.fold_in(arg_keys[8], 71), 0)
    irrep_start = draw_irrep_start(jax.random.fold_in(arg_keys[8], 71), 0)
    return dict(lam=lam, cycle=cycle, eps_occ=eps_occ, eps_vir=eps_vir, occ_irrep=occ_irrep, slab=slab, pair_occ=pair_occ, irrep_start=irrep_start)


def irrep_of(index, starts):
    return jnp.sum((index[:, None] >= starts[None, :]).astype(jnp.int32), axis=1) - 1


def reference(lam, cycle, eps_occ, eps_vir, occ_irrep, slab, pair_occ, irrep_start):
    prod = jnp.dot(lam, cycle, precision=lax.Precision.HIGHEST, preferred_element_type=jnp.float32)
    rows = jnp.arange(SLAB * V, dtype=jnp.int32)
    cols = jnp.arange(JO * V, dtype=jnp.int32)
    occ_row = slab[rows // V]
    vir_row = rows % V
    occ_col = pair_occ[cols // V]
    vir_col = cols % V
    row_energy = eps_occ[occ_row] - eps_vir[vir_row]
    col_energy = eps_occ[occ_col] - eps_vir[vir_col]
    row_sym = jnp.bitwise_xor(occ_irrep[occ_row], irrep_of(vir_row, irrep_start))
    col_sym = jnp.bitwise_xor(occ_irrep[occ_col], irrep_of(vir_col, irrep_start))
    allowed = row_sym[:, None] == col_sym[None, :]
    denom = row_energy[:, None] + col_energy[None, :]
    return jnp.where(allowed, prod / denom, jnp.float32(0.0))
```

```python
import jax
import jax.numpy as jnp
from jax import lax
from jax.experimental import pallas as pl
from jax.experimental.pallas import tpu as pltpu
from jax.sharding import PartitionSpec as P

V = 1200
MESH = pl.DeviceIdType.MESH
NX, NY, NZ = 4, 8, 8
AR, BR = 232, 312
AT, BT = 3, 4
KS = 75
KP = 80
KW = 256
M, MP = 900, 912
N, NP = 750, 768
F32, BF16, I32 = jnp.float32, jnp.bfloat16, jnp.int32


def ahead(i, n):
    return i + 2 if 0 < i and i + 2 < n else None


def sends(event):
    kind, i, j = event
    out = []
    if kind == "A":
        if i == 0:
            if j == 0:
                out += [("xL", ("A", 0, 1)), ("xS", ("A", 0, 2))]
            elif j == 1:
                out += [("xL", ("A", 0, 3))]
            out += [("zL", ("A", 1, j)), ("zS", ("A", 2, j))]
        elif ahead(i, NZ):
            out.append(("zL" if i % 2 else "zS", ("A", i + 2, j)))
    elif kind == "B":
        if j == 0:
            if i == 0:
                out += [("zL", ("B", 1, 0)), ("zS", ("B", 2, 0))]
            elif ahead(i, NZ):
                out.append(("zL" if i % 2 else "zS", ("B", i + 2, 0)))
            out += [("xL", ("B", i, 1)), ("xS", ("B", i, 2))]
        elif j == 1:
            out.append(("xL", ("B", i, 3)))
    elif kind == "C" and j == 0:
        if i == 0:
            out += [("yL", ("C", 1, 0)), ("yS", ("C", 2, 0))]
        elif ahead(i, NY):
            out.append(("yL" if i % 2 else "yS", ("C", i + 2, 0)))
        out.append(("core", ("C", i, 1)))
    return out


def arrivals():
    size = {"A": AR * 512, "B": BR * 512, "C": 2 * KP * NP * 4}
    free = {"x": 0.0, "y": 0.0, "z": 0.0, "c": 0.0}
    waiting = [(0.0, 0, ("B", 0, 0)), (0.0, 1, ("A", 0, 0)), (0.0, 2, ("C", 0, 0))]
    count, order = 3, []
    while waiting:
        waiting.sort()
        now, _, event = waiting.pop(0)
        order.append(event)
        for way, new in sends(event):
            axis = way[0]
            rate = 6e5 if axis == "c" else 1e5
            free[axis] = max(free[axis], now) + size[new[0]] / rate
            waiting.append((free[axis] + 1.0, count, new))
            count += 1
    return order


ORDER = arrivals()
OWN = (("B", 0, 0), ("A", 0, 0), ("C", 0, 0))
INDEX = {e: k for k, e in enumerate(e for e in ORDER if e not in OWN)}


def hop(i):
    return jnp.where(lax.rem(i, 2) == 1, (i + 1) // 2, -(i // 2))


def choose(t, values):
    out = jnp.int32(values[0])
    for k, v in enumerate(values[1:], 1):
        out = jnp.where(t == k, jnp.int32(v), out)
    return out


def kernel(lam_ref, cyc_in, ev_ref, eo_ref, oi_ref, slab_ref, pair_ref, start_ref,
           out_ref, bufa, bufb, cyc, lhs, rhs, acc, recip, evs, rowe, tile,
           send_sem, recv_sem):
    row, col = lax.axis_index("row"), lax.axis_index("col")
    y, core = row // 2, lax.rem(row, 2)
    x, z = col // NZ, lax.rem(col, NZ)
    s = 1 - 2 * core

    def xz(dx, dz):
        return (row, lax.rem(x + dx + NX, NX) * NZ + lax.rem(z + dz + NZ, NZ))

    def yc(dy, c):
        return (lax.rem(y + dy + NY, NY) * 2 + c, col)

    target = {
        "xL": xz(s, 0), "xS": xz(-s, 0), "zL": xz(0, s), "zS": xz(0, -s),
        "yL": yc(s, core), "yS": yc(-s, core), "core": yc(0, 1 - core),
    }

    barrier = pltpu.get_barrier_semaphore()
    for where in target.values():
        pl.semaphore_signal(barrier, inc=1, device_id=where, device_id_type=MESH)

    def place(event):
        kind, i, j = event
        return {"A": bufa, "B": bufb, "C": cyc}[kind].at[i, j]

    def copy(way, source, event):
        k = INDEX[event]
        return pltpu.make_async_remote_copy(
            src_ref=place(source), dst_ref=place(event),
            send_sem=send_sem.at[k], recv_sem=recv_sem.at[k],
            device_id=target[way], device_id_type=MESH,
        )

    came = {}
    for event in ORDER:
        for way, new in sends(event):
            came[new] = (way, event)

    def forward(event):
        for way, new in sends(event):
            copy(way, event, new).start()

    lanes = lax.broadcasted_iota(I32, (8, 128), 1)
    bufb[0, 0, 296:312, :] = jnp.zeros((16, 128), F32)
    for t in range(BT):
        bufb[0, 0, t * KS:(t + 1) * KS, :] = lam_ref[:, (AT + t) * 128:(AT + t + 1) * 128]
    tile[...] = jnp.zeros((128, 128), F32)
    tile[0:KS, 0:4] = lam_ref[:, 896:900]
    rem = tile[...].T[0:8, :]
    r80 = pltpu.roll(rem, 80, 1)
    bufb[0, 0, 304:308, :] = jnp.where(lanes < 80, rem, r80)[0:4]
    bufb[0, 0, 308:312, :] = jnp.where(lanes < 32, r80, pltpu.roll(rem, 32, 1))[0:4]
    bufa[0, 0, 224:232, :] = jnp.zeros((8, 128), F32)
    for t in range(AT):
        bufa[0, 0, t * KS:(t + 1) * KS, :] = lam_ref[:, t * 128:(t + 1) * 128]
    cyc[0, 0, :, 72:80, :] = jnp.zeros((2, 8, NP), F32)
    cyc[0, 0, :, :, 640:NP] = jnp.zeros((2, KP, 128), F32)
    for half in range(2):
        cyc[0, 0, half, 0:KS, 0:N] = cyc_in[half * KS:(half + 1) * KS, :]

    pl.semaphore_wait(barrier, 7)
    for event in OWN:
        forward(event)

    def prep_cycle(i, j):
        yy = lax.rem(y - s * hop(jnp.int32(i)) * (1 - 2 * j) + NY, NY)
        cc = core if j == 0 else 1 - core
        for half in range(2):
            c = (yy * 2 + cc) * 2 + half
            xx, zz = c // NZ, lax.rem(c, NZ)
            v = cyc[i, j, half]
            hi = v.astype(BF16)
            lo = (v - hi.astype(F32)).astype(BF16)
            for k, part in enumerate((hi, lo, hi)):
                at = pl.multiple_of(xx * KW + k * KP, 16)
                rhs[zz, pl.ds(at, KP), :] = part

    def stack(v):
        hi = v.astype(BF16).astype(F32)
        lo = v - hi
        pad = jnp.zeros((KW - 3 * KP, 128), F32)
        return jnp.concatenate([hi, hi, lo, pad], axis=0).T.astype(BF16)

    def prep_lam(iz, ix):
        xx = lax.rem(x - s * hop(ix) + NX, NX)
        at = pl.ds(pl.multiple_of(xx * KW, KW), KW)
        for t in range(AT):
            lhs[iz, t * 128:(t + 1) * 128, at] = stack(bufa[iz, ix, t * KS:t * KS + KP, :])
        for t in range(BT):
            m = (AT + t) * 128
            lhs[iz, m:m + 128, at] = stack(bufb[iz, ix, t * KS:t * KS + KP, :])
        v = bufb[iz, ix, 304:312, :]
        hi = v.astype(BF16).astype(F32)
        rows = lax.broadcasted_iota(I32, (8, 128), 0)
        w = jnp.where((rows < 4) | (lanes < 32), hi, v - hi)
        two = jnp.concatenate([w, pltpu.roll(w, 4, 0)], axis=1)
        lhs[iz, 896:912, at] = jnp.concatenate([two, jnp.zeros((8, KW), F32)], axis=0).astype(BF16)

    def prep_many(shards):
        def one(t, carry):
            prep_lam(choose(t, [a for a, _ in shards]), choose(t, [b for _, b in shards]))
            return carry
        lax.fori_loop(0, len(shards), one, 0)

    def irrep_of(index):
        count = jnp.zeros(index.shape, I32)
        for k in range(8):
            count += (index >= start_ref[k]).astype(I32)
        return count - 1

    def scales():
        for zz in range(NZ):
            for xx in range(NX):
                rhs[zz, xx * KW + 3 * KP:(xx + 1) * KW, :] = jnp.zeros((KW - 3 * KP, NP), BF16)
        evs[...] = jnp.zeros((8, 1280), F32)
        evs[:, 0:V] = jnp.broadcast_to(ev_ref[...], (8, V))

        def turned(first, width):
            e = evs[...]
            at = lax.broadcasted_iota(I32, (8, 1280), 1) + first
            r1 = pltpu.roll(e, lax.rem(1280 - first, 1280), 1)
            r2 = pltpu.roll(e, V - first, 1)
            return jnp.where(at < V, r1, r2)[:, 0:width]

        first_row = lax.rem(row * M, V)
        i0 = row * M // V
        i1 = jnp.minimum(i0 + 1, 11)
        s0, s1 = slab_ref[i0], slab_ref[i1]
        first_col = lax.rem(col * N, V)
        j0 = col * N // V
        j1 = jnp.minimum(j0 + 1, 19)
        p0, p1 = pair_ref[j0], pair_ref[j1]

        rv = turned(first_row, 1024)
        at = lax.broadcasted_iota(I32, (8, 1024), 1) + first_row
        rv = jnp.where(at < V, eo_ref[s0], eo_ref[s1]) - rv
        for t in range(8):
            block = jnp.broadcast_to(rv[0:1, t * 128:(t + 1) * 128], (128, 128)).T
            rowe[t * 128:(t + 1) * 128, :] = block

        at = lax.broadcasted_iota(I32, (8, NP), 1) + first_col
        ce = jnp.where(at < V, eo_ref[p0], eo_ref[p1]) - turned(first_col, NP)
        cs = jnp.where(at < V, oi_ref[p0], oi_ref[p1]) ^ irrep_of(jnp.where(at < V, at, at - V))

        def some(k, carry):
            r = pl.multiple_of(k * 16, 16)
            at = lax.broadcasted_iota(I32, (16, 128), 0) + r + first_row
            rs = jnp.where(at < V, oi_ref[s0], oi_ref[s1]) ^ irrep_of(jnp.where(at < V, at, at - V))
            re = rowe[pl.ds(r, 16), :]
            for t in range(NP // 128):
                part = slice(t * 128, (t + 1) * 128)
                denom = re + jnp.broadcast_to(ce[0:1, part], (16, 128))
                same = rs == jnp.broadcast_to(cs[0:1, part], (16, 128))
                recip[pl.ds(r, 16), part] = jnp.where(same, 1.0 / denom, 0.0)
            return carry
        lax.fori_loop(0, MP // 16, some, 0)
        acc[...] = jnp.zeros((MP, NP), F32)

    def multiply(iz):
        zz = lax.rem(z - s * hop(iz) + NZ, NZ)

        def one(n, carry):
            part = pl.ds(pl.multiple_of(n * 256, 256), 256)
            acc[:, part] += jnp.dot(lhs[iz], rhs[zz, :, part], preferred_element_type=F32)
            return carry
        lax.fori_loop(0, NP // 256, one, 0)

    prep_cycle(0, 0)
    scales()

    arrived, ready, done, left = set(), [], [], 16
    arrived.update({("A", 0, 0), ("B", 0, 0)})
    ready.append((0, 0))
    left -= 1
    prepared, multiplied = set(), 0
    for event in ORDER:
        if event in OWN:
            continue
        way, source = came[event]
        copy(way, source, event).wait_recv()
        forward(event)
        kind, i, j = event
        if kind == "C":
            prep_cycle(i, j)
            left -= 1
        else:
            arrived.add(event)
            if ("A", i, j) in arrived and ("B", i, j) in arrived:
                ready.append((i, j))
        if len(ready) >= 2 or len(prepared) + len(ready) == 32 or (ready and left == 0):
            if ready:
                prep_many(ready)
                prepared.update(ready)
                ready = []
        if left == 0:
            first = multiplied
            while multiplied < NZ and all((multiplied, k) in prepared for k in range(NX)):
                multiplied += 1
            if multiplied > first:
                lax.fori_loop(first, multiplied, lambda k, c: (multiply(k), c)[1], 0)

    def finish(k, carry):
        r = pl.ds(pl.multiple_of(k * 48, 8), 48)
        out_ref[r, :] = (acc[r, :] * recip[r, :])[:, 0:N]
        return carry
    lax.fori_loop(0, 18, finish, 0)
    out_ref[864:900, :] = (acc[864:900, :] * recip[864:900, :])[:, 0:N]

    for event, (way, source) in came.items():
        copy(way, source, event).wait_send()


def local(lam, cycle, eps_occ, eps_vir, occ_irrep, slab, pair_occ, irrep_start):
    vmem = pl.BlockSpec(memory_space=pltpu.VMEM)
    smem = pl.BlockSpec(memory_space=pltpu.SMEM)
    return pl.pallas_call(
        kernel,
        out_shape=jax.ShapeDtypeStruct((M, N), F32),
        in_specs=[vmem, vmem, vmem, smem, smem, smem, smem, smem],
        out_specs=vmem,
        scratch_shapes=[
            pltpu.VMEM((NZ, NX, AR, 128), F32),
            pltpu.VMEM((NZ, NX, BR, 128), F32),
            pltpu.VMEM((NY, 2, 2, KP, NP), F32),
            pltpu.VMEM((NZ, MP, NX * KW), BF16),
            pltpu.VMEM((NZ, NX * KW, NP), BF16),
            pltpu.VMEM((MP, NP), F32),
            pltpu.VMEM((MP, NP), F32),
            pltpu.VMEM((8, 1280), F32),
            pltpu.VMEM((1024, 128), F32),
            pltpu.VMEM((128, 128), F32),
            pltpu.SemaphoreType.DMA((len(INDEX),)),
            pltpu.SemaphoreType.DMA((len(INDEX),)),
        ],
        compiler_params=pltpu.CompilerParams(
            collective_id=0, has_side_effects=True, vmem_limit_bytes=62 * 1024 * 1024
        ),
        cost_estimate=pl.CostEstimate(
            flops=2 * 3 * M * N * 2400, bytes_accessed=4 * M * N, transcendentals=0
        ),
    )(lam.T, cycle, eps_vir.reshape(1, V), eps_occ, occ_irrep, slab, pair_occ, irrep_start)


def solution(mesh):
    placed = (P("row", "col"), P("row", "col"), P(), P(), P(), P(), P(), P())
    return jax.shard_map(
        local, mesh=mesh, in_specs=placed, out_specs=P("row", "col"), check_vma=False
    )
```

```python
import jax
import jax.numpy as jnp
from jax import lax
from jax.experimental import pallas as pl
from jax.experimental.pallas import tpu as pltpu
from jax.sharding import PartitionSpec as P

V = 1200
MESH = pl.DeviceIdType.MESH
NX, NY, NZ = 4, 8, 8
AR, BR = 216, 320
AT, BT = 3, 4
KA = 72
KS, KP = 75, 80
KW = 256
M, MP = 900, 912
N, NP = 750, 768
F32, BF16, I32 = jnp.float32, jnp.bfloat16, jnp.int32

OWN = (("A", 0, 0, 0), ("B", 0, 0, 0), ("C", 0, 0, 0), ("C", 0, 0, 1))


def source(block):
    kind, i, j, h = block
    if kind == "C" and j == 1:
        return "core", (kind, i, 0, h)
    along_x = j > 0 if kind == "B" else j > 0 and i == 0
    if along_x and kind != "C":
        return ("xL" if j % 2 else "xS"), (kind, i, max(j - 2, 0), h)
    axis = "y" if kind == "C" else "z"
    return axis + ("L" if i % 2 else "S"), (kind, max(i - 2, 0), j, h)


SCHEDULE = (
    (None, (("B", 0, 1, 0), ("C", 1, 0, 0), ("B", 1, 0, 0), ("C", 0, 1, 0), ("B", 0, 2, 0), ("B", 2, 0, 0), ("C", 2, 0, 0), ("A", 0, 1, 0), ("C", 1, 0, 1), ("A", 1, 0, 0), ("C", 0, 1, 1), ("A", 0, 2, 0), ("A", 2, 0, 0), ("C", 2, 0, 1), )),
    (("B", 1, 0, 0), (("B", 1, 1, 0), ("B", 3, 0, 0), ("B", 1, 2, 0), )),
    (("B", 0, 1, 0), (("B", 0, 3, 0), )),
    (("C", 1, 0, 0), (("C", 3, 0, 0), ("C", 1, 1, 0), )),
    (("C", 0, 1, 0), ()),
    (("B", 2, 0, 0), (("B", 2, 1, 0), ("B", 2, 2, 0), ("B", 4, 0, 0), )),
    (("B", 0, 2, 0), ()),
    (("A", 0, 1, 0), (("A", 0, 3, 0), ("A", 1, 1, 0), ("A", 2, 1, 0), )),
    (("A", 1, 0, 0), (("A", 3, 0, 0), )),
    (("C", 2, 0, 0), (("C", 2, 1, 0), ("C", 4, 0, 0), )),
    (("C", 0, 1, 1), ()),
    (("A", 0, 2, 0), (("A", 1, 2, 0), ("A", 2, 2, 0), )),
    (("A", 2, 0, 0), (("A", 4, 0, 0), )),
    (("B", 3, 0, 0), (("B", 3, 1, 0), ("B", 5, 0, 0), ("B", 3, 2, 0), )),
    (("B", 1, 1, 0), (("B", 1, 3, 0), )),
    (("C", 1, 0, 1), (("C", 3, 0, 1), ("C", 1, 1, 1), )),
    (("C", 1, 1, 0), ()),
    (("B", 1, 2, 0), ()),
    (("B", 4, 0, 0), (("B", 4, 1, 0), ("B", 4, 2, 0), ("B", 6, 0, 0), )),
    (("C", 2, 0, 1), (("C", 2, 1, 1), ("C", 4, 0, 1), )),
    (("C", 2, 1, 0), ()),
    (("A", 1, 1, 0), (("A", 3, 1, 0), )),
    (("B", 0, 3, 0), ()),
    (("A", 2, 1, 0), (("A", 4, 1, 0), )),
    (("B", 2, 1, 0), (("B", 2, 3, 0), )),
    (("A", 3, 0, 0), (("A", 5, 0, 0), )),
    (("C", 3, 0, 0), (("C", 5, 0, 0), ("C", 3, 1, 0), )),
    (("C", 1, 1, 1), ()),
    (("A", 1, 2, 0), (("A", 3, 2, 0), )),
    (("B", 2, 2, 0), ()),
    (("A", 2, 2, 0), (("A", 4, 2, 0), )),
    (("C", 4, 0, 0), (("C", 4, 1, 0), ("C", 6, 0, 0), )),
    (("C", 2, 1, 1), ()),
    (("A", 0, 3, 0), (("A", 1, 3, 0), ("A", 2, 3, 0), )),
    (("A", 4, 0, 0), (("A", 6, 0, 0), )),
    (("B", 3, 1, 0), (("B", 3, 3, 0), )),
    (("B", 5, 0, 0), (("B", 5, 1, 0), ("B", 7, 0, 0), ("B", 5, 2, 0), )),
    (("C", 3, 0, 1), (("C", 5, 0, 1), ("C", 3, 1, 1), )),
    (("C", 3, 1, 0), ()),
    (("B", 3, 2, 0), ()),
    (("B", 6, 0, 0), (("B", 6, 1, 0), ("B", 6, 2, 0), )),
    (("C", 4, 0, 1), (("C", 4, 1, 1), ("C", 6, 0, 1), )),
    (("C", 4, 1, 0), ()),
    (("B", 1, 3, 0), ()),
    (("A", 3, 1, 0), (("A", 5, 1, 0), )),
    (("A", 4, 1, 0), (("A", 6, 1, 0), )),
    (("B", 4, 1, 0), (("B", 4, 3, 0), )),
    (("A", 5, 0, 0), (("A", 7, 0, 0), )),
    (("C", 5, 0, 0), (("C", 7, 0, 0), ("C", 5, 1, 0), )),
    (("C", 3, 1, 1), ()),
    (("B", 4, 2, 0), ()),
    (("A", 3, 2, 0), (("A", 5, 2, 0), )),
    (("A", 4, 2, 0), (("A", 6, 2, 0), )),
    (("C", 6, 0, 0), (("C", 6, 1, 0), )),
    (("C", 4, 1, 1), ()),
    (("B", 2, 3, 0), ()),
    (("A", 1, 3, 0), (("A", 3, 3, 0), )),
    (("B", 3, 3, 0), ()),
    (("A", 2, 3, 0), (("A", 4, 3, 0), )),
    (("C", 5, 0, 1), (("C", 7, 0, 1), ("C", 5, 1, 1), )),
    (("C", 5, 1, 0), ()),
    (("A", 6, 0, 0), ()),
    (("B", 5, 1, 0), (("B", 5, 3, 0), )),
    (("B", 7, 0, 0), (("B", 7, 1, 0), ("B", 7, 2, 0), )),
    (("C", 6, 0, 1), (("C", 6, 1, 1), )),
    (("C", 6, 1, 0), ()),
    (("B", 5, 2, 0), ()),
    (("A", 5, 1, 0), (("A", 7, 1, 0), )),
    (("B", 6, 1, 0), (("B", 6, 3, 0), )),
    (("A", 6, 1, 0), ()),
    (("C", 7, 0, 0), (("C", 7, 1, 0), )),
    (("C", 5, 1, 1), ()),
    (("A", 7, 0, 0), ()),
    (("B", 6, 2, 0), ()),
    (("A", 5, 2, 0), (("A", 7, 2, 0), )),
    (("C", 7, 0, 1), (("C", 7, 1, 1), )),
    (("C", 6, 1, 1), ()),
    (("B", 4, 3, 0), ()),
    (("A", 6, 2, 0), ()),
    (("A", 3, 3, 0), (("A", 5, 3, 0), )),
    (("B", 5, 3, 0), ()),
    (("C", 7, 1, 0), ()),
    (("A", 4, 3, 0), (("A", 6, 3, 0), )),
    (("B", 7, 1, 0), (("B", 7, 3, 0), )),
    (("A", 7, 1, 0), ()),
    (("A", 7, 2, 0), ()),
    (("C", 7, 1, 1), ()),
    (("B", 7, 2, 0), ()),
    (("A", 5, 3, 0), (("A", 7, 3, 0), )),
    (("B", 6, 3, 0), ()),
    (("A", 6, 3, 0), ()),
    (("A", 7, 3, 0), ()),
    (("B", 7, 3, 0), ()),
)
BLOCKS = [b for b, _ in SCHEDULE[1:]]
INDEX = {b: k for k, b in enumerate(BLOCKS)}


def hop(i):
    return jnp.where(lax.rem(i, 2) == 1, (i + 1) // 2, -(i // 2))


def place_of(distance, n):
    return jnp.where(distance <= n // 2, jnp.maximum(2 * distance - 1, 0), 2 * (n - distance))


def choose(t, values):
    out = jnp.int32(values[0])
    for k, v in enumerate(values[1:], 1):
        out = jnp.where(t == k, jnp.int32(v), out)
    return out


def gather_kernel(lam_ref, cyc_in, ev_ref, eo_ref, oi_ref, slab_ref, pair_ref, start_ref,
                  acc, recip, bufa, bufb, cyc, lhs, rhs, evs, rowe, tile, send_sem, recv_sem):
    row, col = lax.axis_index("row"), lax.axis_index("col")
    y, core = row // 2, lax.rem(row, 2)
    x, z = col // NZ, lax.rem(col, NZ)
    s = 1 - 2 * core

    def xz(dx, dz):
        return (row, lax.rem(x + dx + NX, NX) * NZ + lax.rem(z + dz + NZ, NZ))

    def yc(dy, c):
        return (lax.rem(y + dy + NY, NY) * 2 + c, col)

    target = {
        "xL": xz(s, 0), "xS": xz(-s, 0), "zL": xz(0, s), "zS": xz(0, -s),
        "yL": yc(s, core), "yS": yc(-s, core), "core": yc(0, 1 - core),
    }

    barrier = pltpu.get_barrier_semaphore()
    for where in target.values():
        pl.semaphore_signal(barrier, inc=1, device_id=where, device_id_type=MESH)

    def ref(block):
        kind, i, j, h = block
        return cyc.at[i, j, h] if kind == "C" else {"A": bufa, "B": bufb}[kind].at[i, j]

    def copy(block):
        way, origin = source(block)
        k = INDEX[block]
        return pltpu.make_async_remote_copy(
            src_ref=ref(origin), dst_ref=ref(block),
            send_sem=send_sem.at[k], recv_sem=recv_sem.at[k],
            device_id=target[way], device_id_type=MESH,
        )

    lanes = lax.broadcasted_iota(I32, (8, 128), 1)
    bufb[0, 0, 296:320, :] = jnp.zeros((24, 128), F32)
    for t in range(BT):
        bufb[0, 0, t * KS:(t + 1) * KS, :] = lam_ref[:, (AT + t) * 128:(AT + t + 1) * 128]
    for t in range(AT):
        bufa[0, 0, t * KA:(t + 1) * KA, :] = lam_ref[0:KA, t * 128:(t + 1) * 128]
        bufb[0, 0, 300 + 3 * t:303 + 3 * t, :] = lam_ref[KA:KS, t * 128:(t + 1) * 128]
    tile[...] = jnp.zeros((128, 128), F32)
    tile[0:KS, 0:4] = lam_ref[:, 896:900]
    rem = tile[...].T[0:8, :]
    r80 = pltpu.roll(rem, 80, 1)
    bufb[0, 0, 312:316, :] = jnp.where(lanes < 80, rem, r80)[0:4]
    bufb[0, 0, 316:320, :] = jnp.where(lanes < 32, r80, pltpu.roll(rem, 32, 1))[0:4]
    cyc[0, 0, :, 72:80, :] = jnp.zeros((2, 8, NP), F32)
    cyc[0, 0, :, :, 640:NP] = jnp.zeros((2, KP, 128), F32)
    for half in range(2):
        cyc[0, 0, half, 0:KS, 0:N] = cyc_in[half * KS:(half + 1) * KS, :]

    pl.semaphore_wait(barrier, 7)
    for block in SCHEDULE[0][1]:
        copy(block).start()

    def cycle_shard(i, j, h):
        yy = lax.rem(y - s * hop(jnp.int32(i)) * (1 - 2 * j) + NY, NY)
        return (yy * 2 + (core if j == 0 else 1 - core)) * 2 + h

    def prep_cycle(i, j, h):
        c = cycle_shard(i, j, h)
        v = cyc[i, j, h]
        hi = v.astype(BF16)
        lo = (v - hi.astype(F32)).astype(BF16)
        for k, part in enumerate((hi, lo, hi)):
            rhs[c, k * KP:(k + 1) * KP, :] = part

    def stack(v):
        hi = v.astype(BF16).astype(F32)
        lo = v - hi
        pad = jnp.zeros((KW - 3 * KP, 128), F32)
        return jnp.concatenate([hi, hi, lo, pad], axis=0).T.astype(BF16)

    def prep_lam(iz, ix):
        t4 = iz * NX + ix
        for t in range(AT):
            v = jnp.concatenate(
                [bufa[iz, ix, t * KA:(t + 1) * KA, :], bufb[iz, ix, 300 + 3 * t:308 + 3 * t, :]], axis=0)
            lhs[t4, t * 128:(t + 1) * 128, :] = stack(v)
        for t in range(BT):
            m = (AT + t) * 128
            lhs[t4, m:m + 128, :] = stack(bufb[iz, ix, t * KS:t * KS + KP, :])
        v = bufb[iz, ix, 312:320, :]
        hi = v.astype(BF16).astype(F32)
        rows = lax.broadcasted_iota(I32, (8, 128), 0)
        w = jnp.where((rows < 4) | (lanes < 32), hi, v - hi)
        two = jnp.concatenate([w, pltpu.roll(w, 4, 0)], axis=1)
        lhs[t4, 896:912, :] = jnp.concatenate([two, jnp.zeros((8, KW), F32)], axis=0).astype(BF16)

    def multiply(t4, c):
        acc[...] += jnp.dot(lhs[t4], rhs[c], preferred_element_type=F32)

    def lam_ready(shards, have):
        def one(t, carry):
            iz, ix = choose(t, [a for a, _ in shards]), choose(t, [b for _, b in shards])
            prep_lam(iz, ix)
            c = lax.rem(x - s * hop(ix) + NX, NX) * NZ + lax.rem(z - s * hop(iz) + NZ, NZ)
            if have == (NY, NY):
                multiply(iz * NX + ix, c)
            else:
                other = (lax.rem(c // 2, 2) != core).astype(I32)
                away = s * (y - c // 4) * (1 - 2 * other)
                near = place_of(lax.rem(away + 2 * NY, NY), NY)

                @pl.when(near < jnp.where(other == 1, have[1], have[0]))
                def _():
                    multiply(iz * NX + ix, c)
            return carry
        lax.fori_loop(0, len(shards), one, 0)

    def cycle_ready(i, j, ready):
        def one(h, carry):
            c = cycle_shard(i, j, h)
            ix = place_of(lax.rem(s * (x - c // NZ) + NX, NX), NX)
            iz = place_of(lax.rem(s * (z - lax.rem(c, NZ)) + NZ, NZ), NZ)

            @pl.when(iz < choose(ix, ready))
            def _():
                multiply(iz * NX + ix, c)
            return carry
        if max(ready):
            lax.fori_loop(0, 2, one, 0)

    def irrep_of(index):
        count = jnp.zeros(index.shape, I32)
        for k in range(8):
            count += (index >= start_ref[k]).astype(I32)
        return count - 1

    def scales():
        for c in range(NX * NZ):
            rhs[c, 3 * KP:KW, :] = jnp.zeros((KW - 3 * KP, NP), BF16)
        evs[...] = jnp.zeros((8, 1280), F32)
        evs[:, 0:V] = jnp.broadcast_to(ev_ref[...].reshape(1, V), (8, V))

        def turned(first, width):
            e = evs[...]
            at = lax.broadcasted_iota(I32, (8, 1280), 1) + first
            r1 = pltpu.roll(e, lax.rem(1280 - first, 1280), 1)
            r2 = pltpu.roll(e, V - first, 1)
            return jnp.where(at < V, r1, r2)[:, 0:width]

        first_row = lax.rem(row * M, V)
        i0 = row * M // V
        s0, s1 = slab_ref[i0], slab_ref[jnp.minimum(i0 + 1, 11)]
        first_col = lax.rem(col * N, V)
        j0 = col * N // V
        p0, p1 = pair_ref[j0], pair_ref[jnp.minimum(j0 + 1, 19)]

        rv = turned(first_row, 1024)
        at = lax.broadcasted_iota(I32, (8, 1024), 1) + first_row
        rv = jnp.where(at < V, eo_ref[s0], eo_ref[s1]) - rv
        for t in range(8):
            rowe[t * 128:(t + 1) * 128, :] = jnp.broadcast_to(rv[0:1, t * 128:(t + 1) * 128], (128, 128)).T

        at = lax.broadcasted_iota(I32, (8, NP), 1) + first_col
        ce = jnp.where(at < V, eo_ref[p0], eo_ref[p1]) - turned(first_col, NP)
        cs = jnp.where(at < V, oi_ref[p0], oi_ref[p1]) ^ irrep_of(jnp.where(at < V, at, at - V))

        def some(k, carry):
            r = pl.multiple_of(k * 16, 16)
            at = lax.broadcasted_iota(I32, (16, 128), 0) + r + first_row
            rs = jnp.where(at < V, oi_ref[s0], oi_ref[s1]) ^ irrep_of(jnp.where(at < V, at, at - V))
            re = rowe[pl.ds(r, 16), :]
            for t in range(NP // 128):
                part = slice(t * 128, (t + 1) * 128)
                denom = re + jnp.broadcast_to(ce[0:1, part], (16, 128))
                same = rs == jnp.broadcast_to(cs[0:1, part], (16, 128))
                recip[pl.ds(r, 16), part] = jnp.where(same, 1.0 / denom, 0.0)
                acc[pl.ds(r, 16), part] = jnp.zeros((16, 128), F32)
            return carry
        lax.fori_loop(0, MP // 16, some, 0)

    prep_cycle(0, 0, 0)
    prep_cycle(0, 0, 1)
    scales()

    arrived = set(OWN)
    have = [1, 0]
    ready = [0] * NX
    waiting = []
    todo = [(0, 0)]
    left = NX * NZ

    def flush():
        nonlocal todo, left
        lam_ready(todo, tuple(have))
        for _, b in todo:
            ready[b] += 1
        left -= len(todo)
        todo = []

    for block, issues in SCHEDULE[1:]:
        copy(block).wait_recv()
        for new in issues:
            copy(new).start()
        arrived.add(block)
        kind, i, j, h = block
        if kind == "C":
            prep_cycle(i, j, h)
            while have[j] < NY and all(("C", have[j], j, k) in arrived for k in range(2)):
                cycle_ready(have[j], j, list(ready))
                have[j] += 1
        else:
            pending = [0] * NX
            for _, b in todo:
                pending[b] += 1
            n = ready[j] + pending[j]
            while n < NZ and {("A", n, j, 0), ("B", n, j, 0)} <= arrived:
                todo.append((n, j))
                n += 1
        if len(todo) >= (2 if left > 4 else 1):
            flush()
    assert not todo and left == 0 and have == [NY, NY]

    for block in BLOCKS:
        copy(block).wait_send()


def scale_kernel(acc, recip, out, stage, sem):
    edges = [0, 152, 304, 456, 608, 760, 900]
    copies = []
    for k in range(6):
        rows = pl.ds(edges[k], edges[k + 1] - edges[k])
        stage[rows, :] = (acc[rows, :] * recip[rows, :])[:, 0:N]
        copies.append(pltpu.make_async_copy(stage.at[rows], out.at[rows], sem.at[k]))
        copies[-1].start()
    for c in copies:
        c.wait()


def local(lam, cycle, eps_occ, eps_vir, occ_irrep, slab, pair_occ, irrep_start):
    vmem = pl.BlockSpec(memory_space=pltpu.VMEM)
    smem = pl.BlockSpec(memory_space=pltpu.SMEM)
    acc, recip = pl.pallas_call(
        gather_kernel,
        out_shape=(pltpu.VMEM((MP, NP), F32), pltpu.VMEM((MP, NP), F32)),
        in_specs=[vmem, vmem, vmem, smem, smem, smem, smem, smem],
        out_specs=(vmem, vmem),
        scratch_shapes=[
            pltpu.VMEM((NZ, NX, AR, 128), F32),
            pltpu.VMEM((NZ, NX, BR, 128), F32),
            pltpu.VMEM((NY, 2, 2, KP, NP), F32),
            pltpu.VMEM((NZ * NX, MP, KW), BF16),
            pltpu.VMEM((NZ * NX, KW, NP), BF16),
            pltpu.VMEM((8, 1280), F32),
            pltpu.VMEM((1024, 128), F32),
            pltpu.VMEM((128, 128), F32),
            pltpu.SemaphoreType.DMA((len(INDEX),)),
            pltpu.SemaphoreType.DMA((len(INDEX),)),
        ],
        compiler_params=pltpu.CompilerParams(
            collective_id=0, has_side_effects=True, vmem_limit_bytes=50 * 1024 * 1024
        ),
        cost_estimate=pl.CostEstimate(
            flops=2 * 3 * M * N * 2400, bytes_accessed=4 * M * N, transcendentals=0
        ),
    )(lam.T, cycle, eps_vir, eps_occ, occ_irrep, slab, pair_occ, irrep_start)
    return pl.pallas_call(
        scale_kernel,
        out_shape=jax.ShapeDtypeStruct((M, N), F32),
        in_specs=[vmem, vmem],
        out_specs=pl.BlockSpec(memory_space=pl.ANY),
        scratch_shapes=[pltpu.VMEM((M, N), F32), pltpu.SemaphoreType.DMA((6,))],
        compiler_params=pltpu.CompilerParams(vmem_limit_bytes=8 * 1024 * 1024),
    )(acc, recip)


def solution(mesh):
    placed = (P("row", "col"), P("row", "col"), P(), P(), P(), P(), P(), P())
    return jax.shard_map(
        local, mesh=mesh, in_specs=placed, out_specs=P("row", "col"), check_vma=False
    )
```

```python
import jax
import jax.numpy as jnp
from jax import lax
from jax.experimental import pallas as pl
from jax.experimental.pallas import tpu as pltpu
from jax.sharding import PartitionSpec as P

V = 1200
MESH = pl.DeviceIdType.MESH
NX, NY, NZ = 4, 8, 8
AR, BR = 216, 320
AT, BT = 3, 4
KA = 72
KS, KP = 75, 80
KW = 256
M, MP = 900, 912
N, NP = 750, 768
F32, BF16, I32 = jnp.float32, jnp.bfloat16, jnp.int32

OWN = (("A", 0, 0, 0), ("B", 0, 0, 0), ("C", 0, 0, 0), ("C", 0, 0, 1))


def source(block):
    kind, i, j, h = block
    if kind == "C" and j == 1:
        return "core", (kind, i, 0, h)
    along_x = j > 0 if kind == "B" else j > 0 and i == 0
    if along_x and kind != "C":
        return ("xL" if j % 2 else "xS"), (kind, i, max(j - 2, 0), h)
    axis = "y" if kind == "C" else "z"
    return axis + ("L" if i % 2 else "S"), (kind, max(i - 2, 0), j, h)


SCHEDULE = (
    (None, (("B", 0, 1, 0), ("C", 1, 0, 0), ("B", 1, 0, 0), ("C", 0, 1, 0), ("B", 0, 2, 0), ("B", 2, 0, 0), ("C", 2, 0, 0), ("A", 0, 1, 0), ("C", 1, 0, 1), ("A", 1, 0, 0), ("C", 0, 1, 1), ("A", 0, 2, 0), ("A", 2, 0, 0), ("C", 2, 0, 1), )),
    (("B", 1, 0, 0), (("B", 1, 1, 0), ("B", 3, 0, 0), ("B", 1, 2, 0), )),
    (("B", 0, 1, 0), (("B", 0, 3, 0), )),
    (("C", 1, 0, 0), (("C", 3, 0, 0), ("C", 1, 1, 0), )),
    (("C", 0, 1, 0), ()),
    (("B", 2, 0, 0), (("B", 2, 1, 0), ("B", 2, 2, 0), ("B", 4, 0, 0), )),
    (("B", 0, 2, 0), ()),
    (("A", 0, 1, 0), (("A", 0, 3, 0), ("A", 1, 1, 0), ("A", 2, 1, 0), )),
    (("A", 1, 0, 0), (("A", 3, 0, 0), )),
    (("C", 2, 0, 0), (("C", 2, 1, 0), ("C", 4, 0, 0), )),
    (("C", 0, 1, 1), ()),
    (("A", 0, 2, 0), (("A", 1, 2, 0), ("A", 2, 2, 0), )),
    (("A", 2, 0, 0), (("A", 4, 0, 0), )),
    (("B", 3, 0, 0), (("B", 3, 1, 0), ("B", 5, 0, 0), ("B", 3, 2, 0), )),
    (("B", 1, 1, 0), (("B", 1, 3, 0), )),
    (("C", 1, 0, 1), (("C", 3, 0, 1), ("C", 1, 1, 1), )),
    (("C", 1, 1, 0), ()),
    (("B", 1, 2, 0), ()),
    (("B", 4, 0, 0), (("B", 4, 1, 0), ("B", 4, 2, 0), ("B", 6, 0, 0), )),
    (("C", 2, 0, 1), (("C", 2, 1, 1), ("C", 4, 0, 1), )),
    (("C", 2, 1, 0), ()),
    (("A", 1, 1, 0), (("A", 3, 1, 0), )),
    (("B", 0, 3, 0), ()),
    (("A", 2, 1, 0), (("A", 4, 1, 0), )),
    (("B", 2, 1, 0), (("B", 2, 3, 0), )),
    (("A", 3, 0, 0), (("A", 5, 0, 0), )),
    (("C", 3, 0, 0), (("C", 5, 0, 0), ("C", 3, 1, 0), )),
    (("C", 1, 1, 1), ()),
    (("A", 1, 2, 0), (("A", 3, 2, 0), )),
    (("B", 2, 2, 0), ()),
    (("A", 2, 2, 0), (("A", 4, 2, 0), )),
    (("C", 4, 0, 0), (("C", 4, 1, 0), ("C", 6, 0, 0), )),
    (("C", 2, 1, 1), ()),
    (("A", 0, 3, 0), (("A", 1, 3, 0), ("A", 2, 3, 0), )),
    (("A", 4, 0, 0), (("A", 6, 0, 0), )),
    (("B", 3, 1, 0), (("B", 3, 3, 0), )),
    (("B", 5, 0, 0), (("B", 5, 1, 0), ("B", 7, 0, 0), ("B", 5, 2, 0), )),
    (("C", 3, 0, 1), (("C", 5, 0, 1), ("C", 3, 1, 1), )),
    (("C", 3, 1, 0), ()),
    (("B", 3, 2, 0), ()),
    (("B", 6, 0, 0), (("B", 6, 1, 0), ("B", 6, 2, 0), )),
    (("C", 4, 0, 1), (("C", 4, 1, 1), ("C", 6, 0, 1), )),
    (("C", 4, 1, 0), ()),
    (("B", 1, 3, 0), ()),
    (("A", 3, 1, 0), (("A", 5, 1, 0), )),
    (("A", 4, 1, 0), (("A", 6, 1, 0), )),
    (("B", 4, 1, 0), (("B", 4, 3, 0), )),
    (("A", 5, 0, 0), (("A", 7, 0, 0), )),
    (("C", 5, 0, 0), (("C", 7, 0, 0), ("C", 5, 1, 0), )),
    (("C", 3, 1, 1), ()),
    (("B", 4, 2, 0), ()),
    (("A", 3, 2, 0), (("A", 5, 2, 0), )),
    (("A", 4, 2, 0), (("A", 6, 2, 0), )),
    (("C", 6, 0, 0), (("C", 6, 1, 0), )),
    (("C", 4, 1, 1), ()),
    (("B", 2, 3, 0), ()),
    (("A", 1, 3, 0), (("A", 3, 3, 0), )),
    (("B", 3, 3, 0), ()),
    (("A", 2, 3, 0), (("A", 4, 3, 0), )),
    (("C", 5, 0, 1), (("C", 7, 0, 1), ("C", 5, 1, 1), )),
    (("C", 5, 1, 0), ()),
    (("A", 6, 0, 0), ()),
    (("B", 5, 1, 0), (("B", 5, 3, 0), )),
    (("B", 7, 0, 0), (("B", 7, 1, 0), ("B", 7, 2, 0), )),
    (("C", 6, 0, 1), (("C", 6, 1, 1), )),
    (("C", 6, 1, 0), ()),
    (("B", 5, 2, 0), ()),
    (("A", 5, 1, 0), (("A", 7, 1, 0), )),
    (("B", 6, 1, 0), (("B", 6, 3, 0), )),
    (("A", 6, 1, 0), ()),
    (("C", 7, 0, 0), (("C", 7, 1, 0), )),
    (("C", 5, 1, 1), ()),
    (("A", 7, 0, 0), ()),
    (("B", 6, 2, 0), ()),
    (("A", 5, 2, 0), (("A", 7, 2, 0), )),
    (("C", 7, 0, 1), (("C", 7, 1, 1), )),
    (("C", 6, 1, 1), ()),
    (("B", 4, 3, 0), ()),
    (("A", 6, 2, 0), ()),
    (("A", 3, 3, 0), (("A", 5, 3, 0), )),
    (("B", 5, 3, 0), ()),
    (("C", 7, 1, 0), ()),
    (("A", 4, 3, 0), (("A", 6, 3, 0), )),
    (("B", 7, 1, 0), (("B", 7, 3, 0), )),
    (("A", 7, 1, 0), ()),
    (("A", 7, 2, 0), ()),
    (("C", 7, 1, 1), ()),
    (("B", 7, 2, 0), ()),
    (("A", 5, 3, 0), (("A", 7, 3, 0), )),
    (("B", 6, 3, 0), ()),
    (("A", 6, 3, 0), ()),
    (("A", 7, 3, 0), ()),
    (("B", 7, 3, 0), ()),
)
BLOCKS = [b for b, _ in SCHEDULE[1:]]
INDEX = {b: k for k, b in enumerate(BLOCKS)}


def hop(i):
    return jnp.where(lax.rem(i, 2) == 1, (i + 1) // 2, -(i // 2))


def place_of(distance, n):
    return jnp.where(distance <= n // 2, jnp.maximum(2 * distance - 1, 0), 2 * (n - distance))


def choose(t, values):
    out = jnp.int32(values[0])
    for k, v in enumerate(values[1:], 1):
        out = jnp.where(t == k, jnp.int32(v), out)
    return out


def gather_kernel(lam_ref, cyc_in, ev_ref, eo_ref, oi_ref, slab_ref, pair_ref, start_ref,
                  acc, recip, bufa, bufb, cyc, lhs, rhs, evs, rowe, tile, send_sem, recv_sem):
    row, col = lax.axis_index("row"), lax.axis_index("col")
    y, core = row // 2, lax.rem(row, 2)
    x, z = col // NZ, lax.rem(col, NZ)
    s = 1 - 2 * core

    def xz(dx, dz):
        return (row, lax.rem(x + dx + NX, NX) * NZ + lax.rem(z + dz + NZ, NZ))

    def yc(dy, c):
        return (lax.rem(y + dy + NY, NY) * 2 + c, col)

    target = {
        "xL": xz(s, 0), "xS": xz(-s, 0), "zL": xz(0, s), "zS": xz(0, -s),
        "yL": yc(s, core), "yS": yc(-s, core), "core": yc(0, 1 - core),
    }

    barrier = pltpu.get_barrier_semaphore()
    for where in target.values():
        pl.semaphore_signal(barrier, inc=1, device_id=where, device_id_type=MESH)

    def ref(block):
        kind, i, j, h = block
        return cyc.at[i, j, h] if kind == "C" else {"A": bufa, "B": bufb}[kind].at[i, j]

    def copy(block):
        way, origin = source(block)
        k = INDEX[block]
        return pltpu.make_async_remote_copy(
            src_ref=ref(origin), dst_ref=ref(block),
            send_sem=send_sem.at[k], recv_sem=recv_sem.at[k],
            device_id=target[way], device_id_type=MESH,
        )

    lanes = lax.broadcasted_iota(I32, (8, 128), 1)
    bufb[0, 0, 296:320, :] = jnp.zeros((24, 128), F32)
    for t in range(BT):
        bufb[0, 0, t * KS:(t + 1) * KS, :] = lam_ref[:, (AT + t) * 128:(AT + t + 1) * 128]
    for t in range(AT):
        bufa[0, 0, t * KA:(t + 1) * KA, :] = lam_ref[0:KA, t * 128:(t + 1) * 128]
        bufb[0, 0, 300 + 3 * t:303 + 3 * t, :] = lam_ref[KA:KS, t * 128:(t + 1) * 128]
    tile[...] = jnp.zeros((128, 128), F32)
    tile[0:KS, 0:4] = lam_ref[:, 896:900]
    rem = tile[...].T[0:8, :]
    r80 = pltpu.roll(rem, 80, 1)
    bufb[0, 0, 312:316, :] = jnp.where(lanes < 80, rem, r80)[0:4]
    bufb[0, 0, 316:320, :] = jnp.where(lanes < 32, r80, pltpu.roll(rem, 32, 1))[0:4]
    cyc[0, 0, :, 72:80, :] = jnp.zeros((2, 8, NP), F32)
    cyc[0, 0, :, :, 640:NP] = jnp.zeros((2, KP, 128), F32)
    for half in range(2):
        cyc[0, 0, half, 0:KS, 0:N] = cyc_in[half * KS:(half + 1) * KS, :]

    pl.semaphore_wait(barrier, 7)
    for block in SCHEDULE[0][1]:
        copy(block).start()

    def cycle_shard(i, j, h):
        yy = lax.rem(y - s * hop(jnp.int32(i)) * (1 - 2 * j) + NY, NY)
        return (yy * 2 + (core if j == 0 else 1 - core)) * 2 + h

    def prep_cycle(i, j, h):
        c = cycle_shard(i, j, h)
        v = cyc[i, j, h]
        hi = v.astype(BF16)
        lo = (v - hi.astype(F32)).astype(BF16)
        for k, part in enumerate((hi, lo, hi)):
            rhs[c, k * KP:(k + 1) * KP, :] = part

    def stack(v):
        hi = v.astype(BF16).astype(F32)
        lo = v - hi
        pad = jnp.zeros((KW - 3 * KP, 128), F32)
        return jnp.concatenate([hi, hi, lo, pad], axis=0).T.astype(BF16)

    def prep_a(iz, ix):
        t4 = iz * NX + ix
        for t in range(AT):
            v = jnp.concatenate(
                [bufa[iz, ix, t * KA:(t + 1) * KA, :], bufb[iz, ix, 300 + 3 * t:308 + 3 * t, :]], axis=0)
            lhs[t4, t * 128:(t + 1) * 128, :] = stack(v)

    def prep_b(iz, ix):
        t4 = iz * NX + ix
        for t in range(BT):
            m = (AT + t) * 128
            lhs[t4, m:m + 128, :] = stack(bufb[iz, ix, t * KS:t * KS + KP, :])
        v = bufb[iz, ix, 312:320, :]
        hi = v.astype(BF16).astype(F32)
        rows = lax.broadcasted_iota(I32, (8, 128), 0)
        w = jnp.where((rows < 4) | (lanes < 32), hi, v - hi)
        two = jnp.concatenate([w, pltpu.roll(w, 4, 0)], axis=1)
        lhs[t4, 896:912, :] = jnp.concatenate([two, jnp.zeros((8, KW), F32)], axis=0).astype(BF16)

    def multiply(part, t4, c):
        rows = slice(0, AT * 128) if part == "A" else slice(AT * 128, MP)
        acc[rows, :] += jnp.dot(lhs[t4, rows, :], rhs[c], preferred_element_type=F32)

    def lam_ready(part, iz, ix, have):
        iz, ix = jnp.int32(iz), jnp.int32(ix)
        (prep_a if part == "A" else prep_b)(iz, ix)
        c = lax.rem(x - s * hop(ix) + NX, NX) * NZ + lax.rem(z - s * hop(iz) + NZ, NZ)
        if have == (NY, NY):
            multiply(part, iz * NX + ix, c)
        else:
            other = (lax.rem(c // 2, 2) != core).astype(I32)
            away = s * (y - c // 4) * (1 - 2 * other)
            near = place_of(lax.rem(away + 2 * NY, NY), NY)

            @pl.when(near < jnp.where(other == 1, have[1], have[0]))
            def _():
                multiply(part, iz * NX + ix, c)

    def cycle_ready(i, j, ready):
        def one(h, carry):
            c = cycle_shard(i, j, h)
            ix = place_of(lax.rem(s * (x - c // NZ) + NX, NX), NX)
            iz = place_of(lax.rem(s * (z - lax.rem(c, NZ)) + NZ, NZ), NZ)
            for part in "AB":
                if max(ready[part]):
                    @pl.when(iz < choose(ix, ready[part]))
                    def _():
                        multiply(part, iz * NX + ix, c)
            return carry
        if max(ready["A"] + ready["B"]):
            lax.fori_loop(0, 2, one, 0)

    def irrep_of(index):
        count = jnp.zeros(index.shape, I32)
        for k in range(8):
            count += (index >= start_ref[k]).astype(I32)
        return count - 1

    def scales():
        for c in range(NX * NZ):
            rhs[c, 3 * KP:KW, :] = jnp.zeros((KW - 3 * KP, NP), BF16)
        evs[...] = jnp.zeros((8, 1280), F32)
        evs[:, 0:V] = jnp.broadcast_to(ev_ref[...].reshape(1, V), (8, V))

        def turned(first, width):
            e = evs[...]
            at = lax.broadcasted_iota(I32, (8, 1280), 1) + first
            r1 = pltpu.roll(e, lax.rem(1280 - first, 1280), 1)
            r2 = pltpu.roll(e, V - first, 1)
            return jnp.where(at < V, r1, r2)[:, 0:width]

        first_row = lax.rem(row * M, V)
        i0 = row * M // V
        s0, s1 = slab_ref[i0], slab_ref[jnp.minimum(i0 + 1, 11)]
        first_col = lax.rem(col * N, V)
        j0 = col * N // V
        p0, p1 = pair_ref[j0], pair_ref[jnp.minimum(j0 + 1, 19)]

        rv = turned(first_row, 1024)
        at = lax.broadcasted_iota(I32, (8, 1024), 1) + first_row
        rv = jnp.where(at < V, eo_ref[s0], eo_ref[s1]) - rv
        for t in range(8):
            rowe[t * 128:(t + 1) * 128, :] = jnp.broadcast_to(rv[0:1, t * 128:(t + 1) * 128], (128, 128)).T

        at = lax.broadcasted_iota(I32, (8, NP), 1) + first_col
        ce = jnp.where(at < V, eo_ref[p0], eo_ref[p1]) - turned(first_col, NP)
        cs = jnp.where(at < V, oi_ref[p0], oi_ref[p1]) ^ irrep_of(jnp.where(at < V, at, at - V))

        def some(k, carry):
            r = pl.multiple_of(k * 16, 16)
            at = lax.broadcasted_iota(I32, (16, 128), 0) + r + first_row
            rs = jnp.where(at < V, oi_ref[s0], oi_ref[s1]) ^ irrep_of(jnp.where(at < V, at, at - V))
            re = rowe[pl.ds(r, 16), :]
            for t in range(NP // 128):
                part = slice(t * 128, (t + 1) * 128)
                denom = re + jnp.broadcast_to(ce[0:1, part], (16, 128))
                same = rs == jnp.broadcast_to(cs[0:1, part], (16, 128))
                recip[pl.ds(r, 16), part] = jnp.where(same, 1.0 / denom, 0.0)
                acc[pl.ds(r, 16), part] = jnp.zeros((16, 128), F32)
            return carry
        lax.fori_loop(0, MP // 16, some, 0)

    prep_cycle(0, 0, 0)
    prep_cycle(0, 0, 1)
    scales()

    arrived = set(OWN)
    seen, have = [1, 0], [1, 0]
    here = {"A": [1, 0, 0, 0], "B": [1, 0, 0, 0]}
    ready = {"A": [0] * NX, "B": [0] * NX}
    todo = [("B", 0, 0), ("A", 0, 0)]

    def work(most):
        for kind, i, j in todo[:most]:
            if kind == "C":
                cycle_ready(i, j, {k: list(v) for k, v in ready.items()})
                have[j] += 1
            else:
                lam_ready(kind, i, j, tuple(have))
                ready[kind][j] += 1
        del todo[:most]

    for block, issues in SCHEDULE[1:]:
        copy(block).wait_recv()
        for new in issues:
            copy(new).start()
        arrived.add(block)
        kind, i, j, h = block
        if kind == "C":
            prep_cycle(i, j, h)
            while seen[j] < NY and all(("C", seen[j], j, k) in arrived for k in range(2)):
                todo.append(("C", seen[j], j))
                seen[j] += 1
        else:
            for part in "BA":
                n = here[part]
                while n[j] < NZ and ("B", n[j], j, 0) in arrived and (part, n[j], j, 0) in arrived:
                    todo.append((part, n[j], j))
                    n[j] += 1
        work(1 if len(todo) < 3 else 2)
    work(len(todo))
    assert ready == here and have == [NY, NY]

    for block in BLOCKS:
        copy(block).wait_send()


def scale_kernel(acc, recip, out, stage, sem):
    edges = [0, 152, 304, 456, 608, 760, 900]
    copies = []
    for k in range(6):
        rows = pl.ds(edges[k], edges[k + 1] - edges[k])
        stage[rows, :] = (acc[rows, :] * recip[rows, :])[:, 0:N]
        copies.append(pltpu.make_async_copy(stage.at[rows], out.at[rows], sem.at[k]))
        copies[-1].start()
    for c in copies:
        c.wait()


def local(lam, cycle, eps_occ, eps_vir, occ_irrep, slab, pair_occ, irrep_start):
    vmem = pl.BlockSpec(memory_space=pltpu.VMEM)
    smem = pl.BlockSpec(memory_space=pltpu.SMEM)
    acc, recip = pl.pallas_call(
        gather_kernel,
        out_shape=(pltpu.VMEM((MP, NP), F32), pltpu.VMEM((MP, NP), F32)),
        in_specs=[vmem, vmem, vmem, smem, smem, smem, smem, smem],
        out_specs=(vmem, vmem),
        scratch_shapes=[
            pltpu.VMEM((NZ, NX, AR, 128), F32),
            pltpu.VMEM((NZ, NX, BR, 128), F32),
            pltpu.VMEM((NY, 2, 2, KP, NP), F32),
            pltpu.VMEM((NZ * NX, MP, KW), BF16),
            pltpu.VMEM((NZ * NX, KW, NP), BF16),
            pltpu.VMEM((8, 1280), F32),
            pltpu.VMEM((1024, 128), F32),
            pltpu.VMEM((128, 128), F32),
            pltpu.SemaphoreType.DMA((len(INDEX),)),
            pltpu.SemaphoreType.DMA((len(INDEX),)),
        ],
        compiler_params=pltpu.CompilerParams(
            collective_id=0, has_side_effects=True, vmem_limit_bytes=50 * 1024 * 1024
        ),
        cost_estimate=pl.CostEstimate(
            flops=2 * 3 * M * N * 2400, bytes_accessed=4 * M * N, transcendentals=0
        ),
    )(lam.T, cycle, eps_vir, eps_occ, occ_irrep, slab, pair_occ, irrep_start)
    return pl.pallas_call(
        scale_kernel,
        out_shape=jax.ShapeDtypeStruct((M, N), F32),
        in_specs=[vmem, vmem],
        out_specs=pl.BlockSpec(memory_space=pl.ANY),
        scratch_shapes=[pltpu.VMEM((M, N), F32), pltpu.SemaphoreType.DMA((6,))],
        compiler_params=pltpu.CompilerParams(vmem_limit_bytes=8 * 1024 * 1024),
    )(acc, recip)


def solution(mesh):
    placed = (P("row", "col"), P("row", "col"), P(), P(), P(), P(), P(), P())
    return jax.shard_map(
        local, mesh=mesh, in_specs=placed, out_specs=P("row", "col"), check_vma=False
    )
```

```python
import jax
import jax.numpy as jnp
from jax import lax
from jax.experimental import pallas as pl
from jax.experimental.pallas import tpu as pltpu
from jax.sharding import PartitionSpec as P

V = 1200
MESH = pl.DeviceIdType.MESH
NX, NY, NZ = 4, 8, 8
AR, BR = 216, 320
AT, BT = 3, 4
KA = 72
KS, KP = 75, 80
KW = 256
M, MP = 900, 912
N, NP = 750, 768
LATE = 6
F32, BF16, I32 = jnp.float32, jnp.bfloat16, jnp.int32

OWN = (("A", 0, 0, 0), ("B", 0, 0, 0), ("C", 0, 0, 0), ("C", 0, 0, 1))


def source(block):
    kind, i, j, h = block
    if kind == "C" and j == 1:
        return "core", (kind, i, 0, h)
    along_x = j > 0 if kind == "B" else j > 0 and i == 0
    if along_x and kind != "C":
        return ("xL" if j % 2 else "xS"), (kind, i, max(j - 2, 0), h)
    axis = "y" if kind == "C" else "z"
    return axis + ("L" if i % 2 else "S"), (kind, max(i - 2, 0), j, h)


SCHEDULE = (
    (None, (("B", 0, 1, 0), ("C", 1, 0, 0), ("B", 1, 0, 0), ("C", 0, 1, 0), ("B", 0, 2, 0), ("B", 2, 0, 0), ("C", 2, 0, 0), ("A", 0, 1, 0), ("C", 1, 0, 1), ("A", 1, 0, 0), ("C", 0, 1, 1), ("A", 0, 2, 0), ("A", 2, 0, 0), ("C", 2, 0, 1), )),
    (("B", 1, 0, 0), (("B", 1, 1, 0), ("B", 3, 0, 0), ("B", 1, 2, 0), )),
    (("B", 0, 1, 0), (("B", 0, 3, 0), )),
    (("C", 1, 0, 0), (("C", 3, 0, 0), ("C", 1, 1, 0), )),
    (("C", 0, 1, 0), ()),
    (("B", 2, 0, 0), (("B", 2, 1, 0), ("B", 2, 2, 0), ("B", 4, 0, 0), )),
    (("B", 0, 2, 0), ()),
    (("A", 0, 1, 0), (("A", 0, 3, 0), ("A", 1, 1, 0), ("A", 2, 1, 0), )),
    (("A", 1, 0, 0), (("A", 3, 0, 0), )),
    (("C", 2, 0, 0), (("C", 2, 1, 0), ("C", 4, 0, 0), )),
    (("C", 0, 1, 1), ()),
    (("A", 0, 2, 0), (("A", 1, 2, 0), ("A", 2, 2, 0), )),
    (("A", 2, 0, 0), (("A", 4, 0, 0), )),
    (("B", 3, 0, 0), (("B", 3, 1, 0), ("B", 5, 0, 0), ("B", 3, 2, 0), )),
    (("B", 1, 1, 0), (("B", 1, 3, 0), )),
    (("C", 1, 0, 1), (("C", 3, 0, 1), ("C", 1, 1, 1), )),
    (("C", 1, 1, 0), ()),
    (("B", 1, 2, 0), ()),
    (("B", 4, 0, 0), (("B", 4, 1, 0), ("B", 4, 2, 0), ("B", 6, 0, 0), )),
    (("C", 2, 0, 1), (("C", 2, 1, 1), ("C", 4, 0, 1), )),
    (("C", 2, 1, 0), ()),
    (("A", 1, 1, 0), (("A", 3, 1, 0), )),
    (("B", 0, 3, 0), ()),
    (("A", 2, 1, 0), (("A", 4, 1, 0), )),
    (("B", 2, 1, 0), (("B", 2, 3, 0), )),
    (("A", 3, 0, 0), (("A", 5, 0, 0), )),
    (("C", 3, 0, 0), (("C", 5, 0, 0), ("C", 3, 1, 0), )),
    (("C", 1, 1, 1), ()),
    (("A", 1, 2, 0), (("A", 3, 2, 0), )),
    (("B", 2, 2, 0), ()),
    (("A", 2, 2, 0), (("A", 4, 2, 0), )),
    (("C", 4, 0, 0), (("C", 4, 1, 0), ("C", 6, 0, 0), )),
    (("C", 2, 1, 1), ()),
    (("A", 0, 3, 0), (("A", 1, 3, 0), ("A", 2, 3, 0), )),
    (("A", 4, 0, 0), (("A", 6, 0, 0), )),
    (("B", 3, 1, 0), (("B", 3, 3, 0), )),
    (("B", 5, 0, 0), (("B", 5, 1, 0), ("B", 7, 0, 0), ("B", 5, 2, 0), )),
    (("C", 3, 0, 1), (("C", 5, 0, 1), ("C", 3, 1, 1), )),
    (("C", 3, 1, 0), ()),
    (("B", 3, 2, 0), ()),
    (("B", 6, 0, 0), (("B", 6, 1, 0), ("B", 6, 2, 0), )),
    (("C", 4, 0, 1), (("C", 4, 1, 1), ("C", 6, 0, 1), )),
    (("C", 4, 1, 0), ()),
    (("B", 1, 3, 0), ()),
    (("A", 3, 1, 0), (("A", 5, 1, 0), )),
    (("A", 4, 1, 0), (("A", 6, 1, 0), )),
    (("B", 4, 1, 0), (("B", 4, 3, 0), )),
    (("A", 5, 0, 0), (("A", 7, 0, 0), )),
    (("C", 5, 0, 0), (("C", 7, 0, 0), ("C", 5, 1, 0), )),
    (("C", 3, 1, 1), ()),
    (("B", 4, 2, 0), ()),
    (("A", 3, 2, 0), (("A", 5, 2, 0), )),
    (("A", 4, 2, 0), (("A", 6, 2, 0), )),
    (("C", 6, 0, 0), (("C", 6, 1, 0), )),
    (("C", 4, 1, 1), ()),
    (("B", 2, 3, 0), ()),
    (("A", 1, 3, 0), (("A", 3, 3, 0), )),
    (("B", 3, 3, 0), ()),
    (("A", 2, 3, 0), (("A", 4, 3, 0), )),
    (("C", 5, 0, 1), (("C", 7, 0, 1), ("C", 5, 1, 1), )),
    (("C", 5, 1, 0), ()),
    (("A", 6, 0, 0), ()),
    (("B", 5, 1, 0), (("B", 5, 3, 0), )),
    (("B", 7, 0, 0), (("B", 7, 1, 0), ("B", 7, 2, 0), )),
    (("C", 6, 0, 1), (("C", 6, 1, 1), )),
    (("C", 6, 1, 0), ()),
    (("B", 5, 2, 0), ()),
    (("A", 5, 1, 0), (("A", 7, 1, 0), )),
    (("B", 6, 1, 0), (("B", 6, 3, 0), )),
    (("A", 6, 1, 0), ()),
    (("C", 7, 0, 0), (("C", 7, 1, 0), )),
    (("C", 5, 1, 1), ()),
    (("A", 7, 0, 0), ()),
    (("B", 6, 2, 0), ()),
    (("A", 5, 2, 0), (("A", 7, 2, 0), )),
    (("C", 7, 0, 1), (("C", 7, 1, 1), )),
    (("C", 6, 1, 1), ()),
    (("B", 4, 3, 0), ()),
    (("A", 6, 2, 0), ()),
    (("A", 3, 3, 0), (("A", 5, 3, 0), )),
    (("B", 5, 3, 0), ()),
    (("C", 7, 1, 0), ()),
    (("A", 4, 3, 0), (("A", 6, 3, 0), )),
    (("B", 7, 1, 0), (("B", 7, 3, 0), )),
    (("A", 7, 1, 0), ()),
    (("A", 7, 2, 0), ()),
    (("C", 7, 1, 1), ()),
    (("B", 7, 2, 0), ()),
    (("A", 5, 3, 0), (("A", 7, 3, 0), )),
    (("B", 6, 3, 0), ()),
    (("A", 6, 3, 0), ()),
    (("A", 7, 3, 0), ()),
    (("B", 7, 3, 0), ()),
)
BLOCKS = [b for b, _ in SCHEDULE[1:]]
INDEX = {b: k for k, b in enumerate(BLOCKS)}


def hop(i):
    return jnp.where(lax.rem(i, 2) == 1, (i + 1) // 2, -(i // 2))


def place_of(distance, n):
    return jnp.where(distance <= n // 2, jnp.maximum(2 * distance - 1, 0), 2 * (n - distance))


def choose(t, values):
    out = jnp.int32(values[0])
    for k, v in enumerate(values[1:], 1):
        out = jnp.where(t == k, jnp.int32(v), out)
    return out


def gather_kernel(lam_ref, cyc_in, ev_ref, eo_ref, oi_ref, slab_ref, pair_ref, start_ref,
                  acc, recip, bufa, bufb, cyc, lhs, rhs, evs, rowe, tile, send_sem, recv_sem):
    row, col = lax.axis_index("row"), lax.axis_index("col")
    y, core = row // 2, lax.rem(row, 2)
    x, z = col // NZ, lax.rem(col, NZ)
    s = 1 - 2 * core

    def xz(dx, dz):
        return (row, lax.rem(x + dx + NX, NX) * NZ + lax.rem(z + dz + NZ, NZ))

    def yc(dy, c):
        return (lax.rem(y + dy + NY, NY) * 2 + c, col)

    target = {
        "xL": xz(s, 0), "xS": xz(-s, 0), "zL": xz(0, s), "zS": xz(0, -s),
        "yL": yc(s, core), "yS": yc(-s, core), "core": yc(0, 1 - core),
    }

    barrier = pltpu.get_barrier_semaphore()
    for where in target.values():
        pl.semaphore_signal(barrier, inc=1, device_id=where, device_id_type=MESH)

    def ref(block):
        kind, i, j, h = block
        return cyc.at[i, j, h] if kind == "C" else {"A": bufa, "B": bufb}[kind].at[i, j]

    def copy(block):
        way, origin = source(block)
        k = INDEX[block]
        return pltpu.make_async_remote_copy(
            src_ref=ref(origin), dst_ref=ref(block),
            send_sem=send_sem.at[k], recv_sem=recv_sem.at[k],
            device_id=target[way], device_id_type=MESH,
        )

    lanes = lax.broadcasted_iota(I32, (8, 128), 1)
    bufb[0, 0, 296:320, :] = jnp.zeros((24, 128), F32)
    for t in range(BT):
        bufb[0, 0, t * KS:(t + 1) * KS, :] = lam_ref[:, (AT + t) * 128:(AT + t + 1) * 128]
    for t in range(AT):
        bufa[0, 0, t * KA:(t + 1) * KA, :] = lam_ref[0:KA, t * 128:(t + 1) * 128]
        bufb[0, 0, 300 + 3 * t:303 + 3 * t, :] = lam_ref[KA:KS, t * 128:(t + 1) * 128]
    tile[...] = jnp.zeros((128, 128), F32)
    tile[0:KS, 0:4] = lam_ref[:, 896:900]
    rem = tile[...].T[0:8, :]
    r80 = pltpu.roll(rem, 80, 1)
    bufb[0, 0, 312:316, :] = jnp.where(lanes < 80, rem, r80)[0:4]
    bufb[0, 0, 316:320, :] = jnp.where(lanes < 32, r80, pltpu.roll(rem, 32, 1))[0:4]
    cyc[0, 0, :, 72:80, :] = jnp.zeros((2, 8, NP), F32)
    cyc[0, 0, :, :, 640:NP] = jnp.zeros((2, KP, 128), F32)
    for half in range(2):
        cyc[0, 0, half, 0:KS, 0:N] = cyc_in[half * KS:(half + 1) * KS, :]

    pl.semaphore_wait(barrier, 7)
    for block in SCHEDULE[0][1]:
        copy(block).start()

    def cycle_shard(i, j, h):
        yy = lax.rem(y - s * hop(jnp.int32(i)) * (1 - 2 * j) + NY, NY)
        return (yy * 2 + (core if j == 0 else 1 - core)) * 2 + h

    def prep_cycle(i, j, h):
        c = cycle_shard(i, j, h)
        v = cyc[i, j, h]
        hi = v.astype(BF16)
        lo = (v - hi.astype(F32)).astype(BF16)
        for k, part in enumerate((hi, lo, hi)):
            rhs[c, k * KP:(k + 1) * KP, :] = part

    def stack(v):
        hi = v.astype(BF16).astype(F32)
        lo = v - hi
        pad = jnp.zeros((KW - 3 * KP, 128), F32)
        return jnp.concatenate([hi, hi, lo, pad], axis=0).T.astype(BF16)

    def prep_a(iz, ix):
        t4 = iz * NX + ix
        for t in range(AT):
            v = jnp.concatenate(
                [bufa[iz, ix, t * KA:(t + 1) * KA, :], bufb[iz, ix, 300 + 3 * t:308 + 3 * t, :]], axis=0)
            lhs[t4, t * 128:(t + 1) * 128, :] = stack(v)

    def prep_b(iz, ix):
        t4 = iz * NX + ix
        for t in range(BT):
            m = (AT + t) * 128
            lhs[t4, m:m + 128, :] = stack(bufb[iz, ix, t * KS:t * KS + KP, :])
        v = bufb[iz, ix, 312:320, :]
        hi = v.astype(BF16).astype(F32)
        rows = lax.broadcasted_iota(I32, (8, 128), 0)
        w = jnp.where((rows < 4) | (lanes < 32), hi, v - hi)
        two = jnp.concatenate([w, pltpu.roll(w, 4, 0)], axis=1)
        lhs[t4, 896:912, :] = jnp.concatenate([two, jnp.zeros((8, KW), F32)], axis=0).astype(BF16)

    def multiply(part, t4, c):
        rows = {"A": slice(0, AT * 128), "B": slice(AT * 128, MP), "AB": slice(0, MP)}[part]
        acc[rows, :] += jnp.dot(lhs[t4, rows, :], rhs[c], preferred_element_type=F32)

    def lam_ready(part, iz, ix, have):
        iz, ix = jnp.int32(iz), jnp.int32(ix)
        if "A" in part:
            prep_a(iz, ix)
        if "B" in part:
            prep_b(iz, ix)
        c = lax.rem(x - s * hop(ix) + NX, NX) * NZ + lax.rem(z - s * hop(iz) + NZ, NZ)
        if have == (NY, NY):
            multiply(part, iz * NX + ix, c)
        else:
            other = (lax.rem(c // 2, 2) != core).astype(I32)
            away = s * (y - c // 4) * (1 - 2 * other)
            near = place_of(lax.rem(away + 2 * NY, NY), NY)

            @pl.when(near < jnp.where(other == 1, have[1], have[0]))
            def _():
                multiply(part, iz * NX + ix, c)

    def cycle_ready(i, j, ready):
        def one(h, carry):
            c = cycle_shard(i, j, h)
            ix = place_of(lax.rem(s * (x - c // NZ) + NX, NX), NX)
            iz = place_of(lax.rem(s * (z - lax.rem(c, NZ)) + NZ, NZ), NZ)

            @pl.when(iz < choose(ix, ready))
            def _():
                multiply("AB", iz * NX + ix, c)
            return carry
        if max(ready):
            lax.fori_loop(0, 2, one, 0)

    def irrep_of(index):
        count = jnp.zeros(index.shape, I32)
        for k in range(8):
            count += (index >= start_ref[k]).astype(I32)
        return count - 1

    def scales():
        for c in range(NX * NZ):
            rhs[c, 3 * KP:KW, :] = jnp.zeros((KW - 3 * KP, NP), BF16)
        evs[...] = jnp.zeros((8, 1280), F32)
        evs[:, 0:V] = jnp.broadcast_to(ev_ref[...].reshape(1, V), (8, V))

        def turned(first, width):
            e = evs[...]
            at = lax.broadcasted_iota(I32, (8, 1280), 1) + first
            r1 = pltpu.roll(e, lax.rem(1280 - first, 1280), 1)
            r2 = pltpu.roll(e, V - first, 1)
            return jnp.where(at < V, r1, r2)[:, 0:width]

        first_row = lax.rem(row * M, V)
        i0 = row * M // V
        s0, s1 = slab_ref[i0], slab_ref[jnp.minimum(i0 + 1, 11)]
        first_col = lax.rem(col * N, V)
        j0 = col * N // V
        p0, p1 = pair_ref[j0], pair_ref[jnp.minimum(j0 + 1, 19)]

        rv = turned(first_row, 1024)
        at = lax.broadcasted_iota(I32, (8, 1024), 1) + first_row
        rv = jnp.where(at < V, eo_ref[s0], eo_ref[s1]) - rv
        for t in range(8):
            rowe[t * 128:(t + 1) * 128, :] = jnp.broadcast_to(rv[0:1, t * 128:(t + 1) * 128], (128, 128)).T

        at = lax.broadcasted_iota(I32, (8, NP), 1) + first_col
        ce = jnp.where(at < V, eo_ref[p0], eo_ref[p1]) - turned(first_col, NP)
        cs = jnp.where(at < V, oi_ref[p0], oi_ref[p1]) ^ irrep_of(jnp.where(at < V, at, at - V))

        def some(k, carry):
            r = pl.multiple_of(k * 16, 16)
            at = lax.broadcasted_iota(I32, (16, 128), 0) + r + first_row
            rs = jnp.where(at < V, oi_ref[s0], oi_ref[s1]) ^ irrep_of(jnp.where(at < V, at, at - V))
            re = rowe[pl.ds(r, 16), :]
            for t in range(NP // 128):
                part = slice(t * 128, (t + 1) * 128)
                denom = re + jnp.broadcast_to(ce[0:1, part], (16, 128))
                same = rs == jnp.broadcast_to(cs[0:1, part], (16, 128))
                recip[pl.ds(r, 16), part] = jnp.where(same, 1.0 / denom, 0.0)
                acc[pl.ds(r, 16), part] = jnp.zeros((16, 128), F32)
            return carry
        lax.fori_loop(0, MP // 16, some, 0)

    prep_cycle(0, 0, 0)
    prep_cycle(0, 0, 1)
    scales()

    arrived = set(OWN)
    seen, have = [1, 0], [1, 0]
    here = {"A": [1, 0, 0, 0], "B": [1, 0, 0, 0]}
    ready = {"A": [0] * NX, "B": [0] * NX}
    whole = 1
    todo = [("AB", 0, 0)]

    def work(most):
        for kind, i, j in todo[:most]:
            if kind == "C":
                assert ready["A"] == ready["B"]
                cycle_ready(i, j, list(ready["A"]))
                have[j] += 1
            else:
                lam_ready(kind, i, j, tuple(have))
                for part in kind:
                    ready[part][j] += 1
        del todo[:most]

    for block, issues in SCHEDULE[1:]:
        copy(block).wait_recv()
        for new in issues:
            copy(new).start()
        arrived.add(block)
        kind, i, j, h = block
        if kind == "C":
            prep_cycle(i, j, h)
            while seen[j] < NY and all(("C", seen[j], j, k) in arrived for k in range(2)):
                todo.append(("C", seen[j], j))
                seen[j] += 1
        else:
            late = whole >= NX * NZ - LATE and seen == [NY, NY]
            if not late:
                n, m = here["A"], here["B"]
                while n[j] < NZ and ("A", n[j], j, 0) in arrived and ("B", n[j], j, 0) in arrived:
                    todo.append(("AB", n[j], j))
                    n[j] += 1
                    m[j] += 1
                    whole += 1
            else:
                for k in range(NX):
                    for part in "BA":
                        n = here[part]
                        while n[k] < NZ and ("B", n[k], k, 0) in arrived and (part, n[k], k, 0) in arrived:
                            todo.append((part, n[k], k))
                            n[k] += 1
        work(1 if len(todo) < 3 else 2)
    work(len(todo))
    assert ready == here == {"A": [NZ] * NX, "B": [NZ] * NX} and have == [NY, NY]

    for block in BLOCKS:
        copy(block).wait_send()


def scale_kernel(acc, recip, out, stage, sem):
    edges = [0, 152, 304, 456, 608, 760, 900]
    copies = []
    for k in range(6):
        rows = pl.ds(edges[k], edges[k + 1] - edges[k])
        stage[rows, :] = (acc[rows, :] * recip[rows, :])[:, 0:N]
        copies.append(pltpu.make_async_copy(stage.at[rows], out.at[rows], sem.at[k]))
        copies[-1].start()
    for c in copies:
        c.wait()


def local(lam, cycle, eps_occ, eps_vir, occ_irrep, slab, pair_occ, irrep_start):
    vmem = pl.BlockSpec(memory_space=pltpu.VMEM)
    smem = pl.BlockSpec(memory_space=pltpu.SMEM)
    acc, recip = pl.pallas_call(
        gather_kernel,
        out_shape=(pltpu.VMEM((MP, NP), F32), pltpu.VMEM((MP, NP), F32)),
        in_specs=[vmem, vmem, vmem, smem, smem, smem, smem, smem],
        out_specs=(vmem, vmem),
        scratch_shapes=[
            pltpu.VMEM((NZ, NX, AR, 128), F32),
            pltpu.VMEM((NZ, NX, BR, 128), F32),
            pltpu.VMEM((NY, 2, 2, KP, NP), F32),
            pltpu.VMEM((NZ * NX, MP, KW), BF16),
            pltpu.VMEM((NZ * NX, KW, NP), BF16),
            pltpu.VMEM((8, 1280), F32),
            pltpu.VMEM((1024, 128), F32),
            pltpu.VMEM((128, 128), F32),
            pltpu.SemaphoreType.DMA((len(INDEX),)),
            pltpu.SemaphoreType.DMA((len(INDEX),)),
        ],
        compiler_params=pltpu.CompilerParams(
            collective_id=0, has_side_effects=True, vmem_limit_bytes=50 * 1024 * 1024
        ),
        cost_estimate=pl.CostEstimate(
            flops=2 * 3 * M * N * 2400, bytes_accessed=4 * M * N, transcendentals=0
        ),
    )(lam.T, cycle, eps_vir, eps_occ, occ_irrep, slab, pair_occ, irrep_start)
    return pl.pallas_call(
        scale_kernel,
        out_shape=jax.ShapeDtypeStruct((M, N), F32),
        in_specs=[vmem, vmem],
        out_specs=pl.BlockSpec(memory_space=pl.ANY),
        scratch_shapes=[pltpu.VMEM((M, N), F32), pltpu.SemaphoreType.DMA((6,))],
        compiler_params=pltpu.CompilerParams(vmem_limit_bytes=8 * 1024 * 1024),
    )(acc, recip)


def solution(mesh):
    placed = (P("row", "col"), P("row", "col"), P(), P(), P(), P(), P(), P())
    return jax.shard_map(
        local, mesh=mesh, in_specs=placed, out_specs=P("row", "col"), check_vma=False
    )
```

```python
import jax
import jax.numpy as jnp
from jax import lax
from jax.experimental import pallas as pl
from jax.experimental.pallas import tpu as pltpu
from jax.sharding import PartitionSpec as P

V = 1200
MESH = pl.DeviceIdType.MESH
NX, NY, NZ = 4, 8, 8
AR, BR = 216, 320
AT, BT = 3, 4
KA = 72
KS, KP = 75, 80
KW = 256
M, MP = 900, 912
N, NP = 750, 768
LATE = 6
F32, BF16, I32 = jnp.float32, jnp.bfloat16, jnp.int32

OWN = (("A", 0, 0, 0), ("B", 0, 0, 0), ("C", 0, 0, 0), ("C", 0, 0, 1))


def source(block):
    kind, i, j, h = block
    if kind == "C" and j == 1:
        return "core", (kind, i, 0, h)
    along_x = j > 0 if kind == "B" else j > 0 and i == 0
    if along_x and kind != "C":
        return ("xL" if j % 2 else "xS"), (kind, i, max(j - 2, 0), h)
    axis = "y" if kind == "C" else "z"
    return axis + ("L" if i % 2 else "S"), (kind, max(i - 2, 0), j, h)


SCHEDULE = (
    (None, (("B", 0, 1, 0), ("C", 1, 0, 0), ("B", 1, 0, 0), ("C", 0, 1, 0), ("B", 0, 2, 0), ("B", 2, 0, 0), ("C", 2, 0, 0), ("A", 0, 1, 0), ("C", 1, 0, 1), ("A", 1, 0, 0), ("C", 0, 1, 1), ("A", 0, 2, 0), ("A", 2, 0, 0), ("C", 2, 0, 1), )),
    (("B", 1, 0, 0), (("B", 1, 1, 0), ("B", 3, 0, 0), ("B", 1, 2, 0), )),
    (("B", 0, 1, 0), (("B", 0, 3, 0), )),
    (("C", 1, 0, 0), (("C", 3, 0, 0), ("C", 1, 1, 0), )),
    (("C", 0, 1, 0), ()),
    (("B", 2, 0, 0), (("B", 2, 1, 0), ("B", 2, 2, 0), ("B", 4, 0, 0), )),
    (("B", 0, 2, 0), ()),
    (("A", 0, 1, 0), (("A", 0, 3, 0), ("A", 1, 1, 0), ("A", 2, 1, 0), )),
    (("A", 1, 0, 0), (("A", 3, 0, 0), )),
    (("C", 2, 0, 0), (("C", 2, 1, 0), ("C", 4, 0, 0), )),
    (("C", 0, 1, 1), ()),
    (("A", 0, 2, 0), (("A", 1, 2, 0), ("A", 2, 2, 0), )),
    (("A", 2, 0, 0), (("A", 4, 0, 0), )),
    (("B", 3, 0, 0), (("B", 3, 1, 0), ("B", 5, 0, 0), ("B", 3, 2, 0), )),
    (("B", 1, 1, 0), (("B", 1, 3, 0), )),
    (("C", 1, 0, 1), (("C", 3, 0, 1), ("C", 1, 1, 1), )),
    (("C", 1, 1, 0), ()),
    (("B", 1, 2, 0), ()),
    (("B", 4, 0, 0), (("B", 4, 1, 0), ("B", 4, 2, 0), ("B", 6, 0, 0), )),
    (("C", 2, 0, 1), (("C", 2, 1, 1), ("C", 4, 0, 1), )),
    (("C", 2, 1, 0), ()),
    (("A", 1, 1, 0), (("A", 3, 1, 0), )),
    (("B", 0, 3, 0), ()),
    (("A", 2, 1, 0), (("A", 4, 1, 0), )),
    (("B", 2, 1, 0), (("B", 2, 3, 0), )),
    (("A", 3, 0, 0), (("A", 5, 0, 0), )),
    (("C", 3, 0, 0), (("C", 5, 0, 0), ("C", 3, 1, 0), )),
    (("C", 1, 1, 1), ()),
    (("A", 1, 2, 0), (("A", 3, 2, 0), )),
    (("B", 2, 2, 0), ()),
    (("A", 2, 2, 0), (("A", 4, 2, 0), )),
    (("C", 4, 0, 0), (("C", 4, 1, 0), ("C", 6, 0, 0), )),
    (("C", 2, 1, 1), ()),
    (("A", 0, 3, 0), (("A", 1, 3, 0), ("A", 2, 3, 0), )),
    (("A", 4, 0, 0), (("A", 6, 0, 0), )),
    (("B", 3, 1, 0), (("B", 3, 3, 0), )),
    (("B", 5, 0, 0), (("B", 5, 1, 0), ("B", 7, 0, 0), ("B", 5, 2, 0), )),
    (("C", 3, 0, 1), (("C", 5, 0, 1), ("C", 3, 1, 1), )),
    (("C", 3, 1, 0), ()),
    (("B", 3, 2, 0), ()),
    (("B", 6, 0, 0), (("B", 6, 1, 0), ("B", 6, 2, 0), )),
    (("C", 4, 0, 1), (("C", 4, 1, 1), ("C", 6, 0, 1), )),
    (("C", 4, 1, 0), ()),
    (("B", 1, 3, 0), ()),
    (("A", 3, 1, 0), (("A", 5, 1, 0), )),
    (("A", 4, 1, 0), (("A", 6, 1, 0), )),
    (("B", 4, 1, 0), (("B", 4, 3, 0), )),
    (("A", 5, 0, 0), (("A", 7, 0, 0), )),
    (("C", 5, 0, 0), (("C", 7, 0, 0), ("C", 5, 1, 0), )),
    (("C", 3, 1, 1), ()),
    (("B", 4, 2, 0), ()),
    (("A", 3, 2, 0), (("A", 5, 2, 0), )),
    (("A", 4, 2, 0), (("A", 6, 2, 0), )),
    (("C", 6, 0, 0), (("C", 6, 1, 0), )),
    (("C", 4, 1, 1), ()),
    (("B", 2, 3, 0), ()),
    (("A", 1, 3, 0), (("A", 3, 3, 0), )),
    (("B", 3, 3, 0), ()),
    (("A", 2, 3, 0), (("A", 4, 3, 0), )),
    (("C", 5, 0, 1), (("C", 7, 0, 1), ("C", 5, 1, 1), )),
    (("C", 5, 1, 0), ()),
    (("A", 6, 0, 0), ()),
    (("B", 5, 1, 0), (("B", 5, 3, 0), )),
    (("B", 7, 0, 0), (("B", 7, 1, 0), ("B", 7, 2, 0), )),
    (("C", 6, 0, 1), (("C", 6, 1, 1), )),
    (("C", 6, 1, 0), ()),
    (("B", 5, 2, 0), ()),
    (("A", 5, 1, 0), (("A", 7, 1, 0), )),
    (("B", 6, 1, 0), (("B", 6, 3, 0), )),
    (("A", 6, 1, 0), ()),
    (("C", 7, 0, 0), (("C", 7, 1, 0), )),
    (("C", 5, 1, 1), ()),
    (("A", 7, 0, 0), ()),
    (("B", 6, 2, 0), ()),
    (("A", 5, 2, 0), (("A", 7, 2, 0), )),
    (("C", 7, 0, 1), (("C", 7, 1, 1), )),
    (("C", 6, 1, 1), ()),
    (("B", 4, 3, 0), ()),
    (("A", 6, 2, 0), ()),
    (("A", 3, 3, 0), (("A", 5, 3, 0), )),
    (("B", 5, 3, 0), ()),
    (("C", 7, 1, 0), ()),
    (("A", 4, 3, 0), (("A", 6, 3, 0), )),
    (("B", 7, 1, 0), (("B", 7, 3, 0), )),
    (("A", 7, 1, 0), ()),
    (("A", 7, 2, 0), ()),
    (("C", 7, 1, 1), ()),
    (("B", 7, 2, 0), ()),
    (("A", 5, 3, 0), (("A", 7, 3, 0), )),
    (("B", 6, 3, 0), ()),
    (("A", 6, 3, 0), ()),
    (("A", 7, 3, 0), ()),
    (("B", 7, 3, 0), ()),
)
BLOCKS = [b for b, _ in SCHEDULE[1:]]
INDEX = {b: k for k, b in enumerate(BLOCKS)}


def hop(i):
    return jnp.where(lax.rem(i, 2) == 1, (i + 1) // 2, -(i // 2))


def place_of(distance, n):
    return jnp.where(distance <= n // 2, jnp.maximum(2 * distance - 1, 0), 2 * (n - distance))


def choose(t, values):
    out = jnp.int32(values[0])
    for k, v in enumerate(values[1:], 1):
        out = jnp.where(t == k, jnp.int32(v), out)
    return out


def gather_kernel(lam_ref, cyc_in, ev_ref, eo_ref, oi_ref, slab_ref, pair_ref, start_ref,
                  acc, recip, bufa, bufb, cyc, lhs, rhs, evs, rowe, tile, send_sem, recv_sem):
    row, col = lax.axis_index("row"), lax.axis_index("col")
    y, core = row // 2, lax.rem(row, 2)
    x, z = col // NZ, lax.rem(col, NZ)
    s = 1 - 2 * core

    def xz(dx, dz):
        return (row, lax.rem(x + dx + NX, NX) * NZ + lax.rem(z + dz + NZ, NZ))

    def yc(dy, c):
        return (lax.rem(y + dy + NY, NY) * 2 + c, col)

    target = {
        "xL": xz(s, 0), "xS": xz(-s, 0), "zL": xz(0, s), "zS": xz(0, -s),
        "yL": yc(s, core), "yS": yc(-s, core), "core": yc(0, 1 - core),
    }

    barrier = pltpu.get_barrier_semaphore()
    for where in target.values():
        pl.semaphore_signal(barrier, inc=1, device_id=where, device_id_type=MESH)

    def ref(block):
        kind, i, j, h = block
        return cyc.at[i, j, h] if kind == "C" else {"A": bufa, "B": bufb}[kind].at[i, j]

    def copy(block):
        way, origin = source(block)
        k = INDEX[block]
        return pltpu.make_async_remote_copy(
            src_ref=ref(origin), dst_ref=ref(block),
            send_sem=send_sem.at[k], recv_sem=recv_sem.at[k],
            device_id=target[way], device_id_type=MESH,
        )

    lanes = lax.broadcasted_iota(I32, (8, 128), 1)
    bufb[0, 0, 296:320, :] = jnp.zeros((24, 128), F32)
    for t in range(BT):
        bufb[0, 0, t * KS:(t + 1) * KS, :] = lam_ref[:, (AT + t) * 128:(AT + t + 1) * 128]
    for t in range(AT):
        bufa[0, 0, t * KA:(t + 1) * KA, :] = lam_ref[0:KA, t * 128:(t + 1) * 128]
        bufb[0, 0, 300 + 3 * t:303 + 3 * t, :] = lam_ref[KA:KS, t * 128:(t + 1) * 128]
    tile[...] = jnp.zeros((128, 128), F32)
    tile[0:KS, 0:4] = lam_ref[:, 896:900]
    rem = tile[...].T[0:8, :]
    r80 = pltpu.roll(rem, 80, 1)
    bufb[0, 0, 312:316, :] = jnp.where(lanes < 80, rem, r80)[0:4]
    bufb[0, 0, 316:320, :] = jnp.where(lanes < 32, r80, pltpu.roll(rem, 32, 1))[0:4]
    cyc[0, 0, :, 72:80, :] = jnp.zeros((2, 8, NP), F32)
    cyc[0, 0, :, :, 640:NP] = jnp.zeros((2, KP, 128), F32)
    for half in range(2):
        cyc[0, 0, half, 0:KS, 0:N] = cyc_in[half * KS:(half + 1) * KS, :]

    pl.semaphore_wait(barrier, 7)
    for block in SCHEDULE[0][1]:
        copy(block).start()

    def cycle_shard(i, j, h):
        yy = lax.rem(y - s * hop(jnp.int32(i)) * (1 - 2 * j) + NY, NY)
        return (yy * 2 + (core if j == 0 else 1 - core)) * 2 + h

    def prep_cycle(i, j, h):
        c = cycle_shard(i, j, h)
        v = cyc[i, j, h]
        hi = v.astype(BF16)
        lo = (v - hi.astype(F32)).astype(BF16)
        for k, part in enumerate((hi, lo, hi)):
            rhs[c, k * KP:(k + 1) * KP, :] = part

    def stack(v):
        hi = v.astype(BF16).astype(F32)
        lo = v - hi
        pad = jnp.zeros((KW - 3 * KP, 128), F32)
        return jnp.concatenate([hi, hi, lo, pad], axis=0).T.astype(BF16)

    def prep_a(iz, ix):
        t4 = iz * NX + ix
        for t in range(AT):
            v = jnp.concatenate(
                [bufa[iz, ix, t * KA:(t + 1) * KA, :], bufb[iz, ix, 300 + 3 * t:308 + 3 * t, :]], axis=0)
            lhs[t4, t * 128:(t + 1) * 128, :] = stack(v)

    def prep_b(iz, ix):
        t4 = iz * NX + ix
        for t in range(BT):
            m = (AT + t) * 128
            lhs[t4, m:m + 128, :] = stack(bufb[iz, ix, t * KS:t * KS + KP, :])
        v = bufb[iz, ix, 312:320, :]
        hi = v.astype(BF16).astype(F32)
        rows = lax.broadcasted_iota(I32, (8, 128), 0)
        w = jnp.where((rows < 4) | (lanes < 32), hi, v - hi)
        two = jnp.concatenate([w, pltpu.roll(w, 4, 0)], axis=1)
        lhs[t4, 896:912, :] = jnp.concatenate([two, jnp.zeros((8, KW), F32)], axis=0).astype(BF16)

    def multiply(part, t4, c):
        rows = {"A": slice(0, AT * 128), "B": slice(AT * 128, MP), "AB": slice(0, MP)}[part]
        acc[rows, :] += jnp.dot(lhs[t4, rows, :], rhs[c], preferred_element_type=F32)

    def lam_ready(part, iz, ix, have):
        iz, ix = jnp.int32(iz), jnp.int32(ix)
        if "A" in part:
            prep_a(iz, ix)
        if "B" in part:
            prep_b(iz, ix)
        c = lax.rem(x - s * hop(ix) + NX, NX) * NZ + lax.rem(z - s * hop(iz) + NZ, NZ)
        if have == (NY, NY):
            multiply(part, iz * NX + ix, c)
        else:
            other = (lax.rem(c // 2, 2) != core).astype(I32)
            away = s * (y - c // 4) * (1 - 2 * other)
            near = place_of(lax.rem(away + 2 * NY, NY), NY)

            @pl.when(near < jnp.where(other == 1, have[1], have[0]))
            def _():
                multiply(part, iz * NX + ix, c)

    def cycle_ready(i, j, ready):
        def one(h, carry):
            c = cycle_shard(i, j, h)
            ix = place_of(lax.rem(s * (x - c // NZ) + NX, NX), NX)
            iz = place_of(lax.rem(s * (z - lax.rem(c, NZ)) + NZ, NZ), NZ)

            @pl.when(iz < choose(ix, ready))
            def _():
                multiply("AB", iz * NX + ix, c)
            return carry
        if max(ready):
            lax.fori_loop(0, 2, one, 0)

    def irrep_of(index):
        count = jnp.zeros(index.shape, I32)
        for k in range(8):
            count += (index >= start_ref[k]).astype(I32)
        return count - 1

    def scales():
        for c in range(NX * NZ):
            rhs[c, 3 * KP:KW, :] = jnp.zeros((KW - 3 * KP, NP), BF16)
        evs[...] = jnp.zeros((8, 1280), F32)
        evs[:, 0:V] = jnp.broadcast_to(ev_ref[...].reshape(1, V), (8, V))

        def turned(first, width):
            e = evs[...]
            at = lax.broadcasted_iota(I32, (8, 1280), 1) + first
            r1 = pltpu.roll(e, lax.rem(1280 - first, 1280), 1)
            r2 = pltpu.roll(e, V - first, 1)
            return jnp.where(at < V, r1, r2)[:, 0:width]

        first_row = lax.rem(row * M, V)
        i0 = row * M // V
        s0, s1 = slab_ref[i0], slab_ref[jnp.minimum(i0 + 1, 11)]
        first_col = lax.rem(col * N, V)
        j0 = col * N // V
        p0, p1 = pair_ref[j0], pair_ref[jnp.minimum(j0 + 1, 19)]

        rv = turned(first_row, 1024)
        at = lax.broadcasted_iota(I32, (8, 1024), 1) + first_row
        rv = jnp.where(at < V, eo_ref[s0], eo_ref[s1]) - rv
        for t in range(8):
            rowe[t * 128:(t + 1) * 128, :] = jnp.broadcast_to(rv[0:1, t * 128:(t + 1) * 128], (128, 128)).T

        at = lax.broadcasted_iota(I32, (8, NP), 1) + first_col
        ce = jnp.where(at < V, eo_ref[p0], eo_ref[p1]) - turned(first_col, NP)
        cs = jnp.where(at < V, oi_ref[p0], oi_ref[p1]) ^ irrep_of(jnp.where(at < V, at, at - V))

        def some(k, carry):
            r = pl.multiple_of(k * 16, 16)
            at = lax.broadcasted_iota(I32, (16, 128), 0) + r + first_row
            rs = jnp.where(at < V, oi_ref[s0], oi_ref[s1]) ^ irrep_of(jnp.where(at < V, at, at - V))
            re = rowe[pl.ds(r, 16), :]
            for t in range(NP // 128):
                part = slice(t * 128, (t + 1) * 128)
                denom = re + jnp.broadcast_to(ce[0:1, part], (16, 128))
                same = rs == jnp.broadcast_to(cs[0:1, part], (16, 128))
                recip[pl.ds(r, 16), part] = jnp.where(same, 1.0 / denom, 0.0)
                acc[pl.ds(r, 16), part] = jnp.zeros((16, 128), F32)
            return carry
        lax.fori_loop(0, MP // 16, some, 0)

    prep_cycle(0, 0, 0)
    prep_cycle(0, 0, 1)
    scales()

    sent = list(SCHEDULE[0][1])
    arrived = set(OWN)
    seen, have = [1, 0], [1, 0]
    here = {"A": [1, 0, 0, 0], "B": [1, 0, 0, 0]}
    ready = {"A": [0] * NX, "B": [0] * NX}
    whole = 1
    todo = [("AB", 0, 0)]

    def work(most):
        for kind, i, j in todo[:most]:
            if kind == "C":
                assert ready["A"] == ready["B"]
                cycle_ready(i, j, list(ready["A"]))
                have[j] += 1
            else:
                lam_ready(kind, i, j, tuple(have))
                for part in kind:
                    ready[part][j] += 1
        del todo[:most]

    for block, issues in SCHEDULE[1:]:
        copy(block).wait_recv()
        for new in issues:
            copy(new).start()
        sent.extend(issues)
        arrived.add(block)
        kind, i, j, h = block
        if kind == "C":
            prep_cycle(i, j, h)
            while seen[j] < NY and all(("C", seen[j], j, k) in arrived for k in range(2)):
                todo.append(("C", seen[j], j))
                seen[j] += 1
        else:
            late = whole >= NX * NZ - LATE and seen == [NY, NY]
            if not late:
                n, m = here["A"], here["B"]
                while n[j] < NZ and ("A", n[j], j, 0) in arrived and ("B", n[j], j, 0) in arrived:
                    todo.append(("AB", n[j], j))
                    n[j] += 1
                    m[j] += 1
                    whole += 1
            else:
                for k in range(NX):
                    for part in "BA":
                        n = here[part]
                        while n[k] < NZ and ("B", n[k], k, 0) in arrived and (part, n[k], k, 0) in arrived:
                            todo.append((part, n[k], k))
                            n[k] += 1
        work(1 if len(todo) < 3 else 2)
        while len(sent) > 32:
            copy(sent.pop(0)).wait_send()
    work(len(todo))
    assert ready == here == {"A": [NZ] * NX, "B": [NZ] * NX} and have == [NY, NY]

    for block in sent:
        copy(block).wait_send()


def scale_kernel(acc, recip, out, stage, sem):
    edges = [0, 152, 304, 456, 608, 760, 900]
    copies = []
    for k in range(6):
        rows = pl.ds(edges[k], edges[k + 1] - edges[k])
        stage[rows, :] = (acc[rows, :] * recip[rows, :])[:, 0:N]
        copies.append(pltpu.make_async_copy(stage.at[rows], out.at[rows], sem.at[k]))
        copies[-1].start()
    for c in copies:
        c.wait()


def local(lam, cycle, eps_occ, eps_vir, occ_irrep, slab, pair_occ, irrep_start):
    vmem = pl.BlockSpec(memory_space=pltpu.VMEM)
    smem = pl.BlockSpec(memory_space=pltpu.SMEM)
    acc, recip = pl.pallas_call(
        gather_kernel,
        out_shape=(pltpu.VMEM((MP, NP), F32), pltpu.VMEM((MP, NP), F32)),
        in_specs=[vmem, vmem, vmem, smem, smem, smem, smem, smem],
        out_specs=(vmem, vmem),
        scratch_shapes=[
            pltpu.VMEM((NZ, NX, AR, 128), F32),
            pltpu.VMEM((NZ, NX, BR, 128), F32),
            pltpu.VMEM((NY, 2, 2, KP, NP), F32),
            pltpu.VMEM((NZ * NX, MP, KW), BF16),
            pltpu.VMEM((NZ * NX, KW, NP), BF16),
            pltpu.VMEM((8, 1280), F32),
            pltpu.VMEM((1024, 128), F32),
            pltpu.VMEM((128, 128), F32),
            pltpu.SemaphoreType.DMA((len(INDEX),)),
            pltpu.SemaphoreType.DMA((len(INDEX),)),
        ],
        compiler_params=pltpu.CompilerParams(
            collective_id=0, has_side_effects=True, vmem_limit_bytes=50 * 1024 * 1024
        ),
        cost_estimate=pl.CostEstimate(
            flops=2 * 3 * M * N * 2400, bytes_accessed=4 * M * N, transcendentals=0
        ),
    )(lam.T, cycle, eps_vir, eps_occ, occ_irrep, slab, pair_occ, irrep_start)
    return pl.pallas_call(
        scale_kernel,
        out_shape=jax.ShapeDtypeStruct((M, N), F32),
        in_specs=[vmem, vmem],
        out_specs=pl.BlockSpec(memory_space=pl.ANY),
        scratch_shapes=[pltpu.VMEM((M, N), F32), pltpu.SemaphoreType.DMA((6,))],
        compiler_params=pltpu.CompilerParams(vmem_limit_bytes=8 * 1024 * 1024),
    )(acc, recip)


def solution(mesh):
    placed = (P("row", "col"), P("row", "col"), P(), P(), P(), P(), P(), P())
    return jax.shard_map(
        local, mesh=mesh, in_specs=placed, out_specs=P("row", "col"), check_vma=False
    )
```
